32 devices in a mesh: grp: 4 (over y, core), sub: 8 (over z, x).
Axes of the slice: x: 2, y: 2, z: 4, core: 2. Of those that a mesh axis runs over, the one named last changes fastest.
Arguments:
- activations: bfloat16 [16384, 2048], P(('grp', 'sub')), may hold values from -110 to 110
- norm_gain: float32 [2048], replicated, may hold values from 0.5 to 1.5
- key_weight: bfloat16 [2048, 768], P('sub'), may hold values from -0.125 to 0.125
- key_grads: bfloat16 [16384, 768], P(('grp', 'sub')), may hold values from -3 to 3
Outputs:
- input_grads: bfloat16 [16384, 2048], P(('grp', 'sub'))
- weight_grads: float32 [2048, 768], P('sub', 'grp')
- gain_grads: float32 [2048], P('sub')
The draws below stay inside these ranges and needn't reach their ends.
All inputs are finite; a program needn't handle non-finite values.
Results may differ from the reference program's by a relative error of at most 0.0029.
Values may be sent and summed in bfloat16 or wider, within the bound.
No kernel may reach another device: no remote copies, remote signals or barrier semaphores. Data moves between devices by JAX's collectives and lax.ppermute only.
A program may use at most 64 MiB of HBM per device.

```python
import math
import jax
import jax.numpy as jnp
from jax import lax

D = 2048
KW = 768
TOK_DEV = 512
TOKENS = 16384
N_GRP = 4
N_SUB = 8


def draw_activations(key, part):
    key_base, key_rows, key_cols = jax.random.split(key, 3)
    base = jnp.clip(jax.random.normal(key_base, (TOKENS, D), jnp.float32), -4.0, 4.0)
    row_scale = jnp.exp(jax.random.uniform(key_rows, (TOKENS, 1), jnp.float32) * math.log(10.0))
    col_scale = 0.5 * jnp.exp(jax.random.uniform(key_cols, (1, D), jnp.float32) * math.log(4.0))
    return (base * row_scale * col_scale).astype(jnp.bfloat16)


def levels(rng, extent, pieces, least, high):
    level, own = 1.0, jax.random.fold_in(rng, 6)
    for dim, parts in pieces:
        steps = jnp.exp(jax.random.uniform(jax.random.fold_in(own, dim), (parts,), jnp.float32, least / len(pieces), high / len(pieces)))
        level = level * jnp.repeat(steps, extent[dim] // parts).reshape([-1 if axis == dim else 1 for axis in range(len(extent))])
    return level


def scatter_about(key, dims, deviation, bound, shards=(), dtype=jnp.bfloat16):
    entries = deviation * jax.random.normal(key, dims, jnp.float32)
    if shards:
        entries = entries * levels(key, dims, shards, -0.22, 0.18)
    return jnp.clip(entries, -bound, bound).astype(dtype)


def setup_inputs(seed: int = 0) -> dict:
    seeds = jax.random.split(jax.random.key(seed), 5)
    activations = draw_activations(jax.random.fold_in(seeds[4], 71), 0)
    norm_gain = jnp.clip(jax.random.uniform(seeds[1], (D,), jnp.float32, 0.5, 1.5), 0.5, 1.5)
    key_weight = scatter_about(seeds[2], (D, KW), D ** -0.5, 0.125, ((0, 8),))
    key_grads = scatter_about(seeds[3], (TOKENS, KW), 0.5, 3.0, ((0, 32),))
    return {"activations": activations, "norm_gain": norm_gain, "key_weight": key_weight, "key_grads": key_grads}


def reference(activations, norm_gain, key_weight, key_grads):
    inputs = activations.astype(jnp.float32)
    mean_square = lax.optimization_barrier(jnp.mean(inputs * inputs, axis=1, keepdims=True))
    inverse_rms = lax.rsqrt(mean_square + 1e-05)
    normed = inputs * inverse_rms
    scaled = (normed * norm_gain).astype(jnp.bfloat16)
    grad_scaled = jnp.dot(key_grads, key_weight.T, preferred_element_type=jnp.float32)
    gained = norm_gain * grad_scaled
    input_grads = (inverse_rms * (gained - normed * lax.optimization_barrier(jnp.mean(gained * normed, axis=1, keepdims=True)))).astype(jnp.bfloat16)
    groups = N_GRP
    gain_grads = lax.optimization_barrier(jnp.sum(grad_scaled * normed, axis=0)) / groups
    blocks = N_GRP * N_SUB
    scaled_blocks = scaled.reshape(blocks, TOK_DEV, D)
    grad_blocks = key_grads.reshape(blocks, TOK_DEV, KW)

    def add_block(total, pair):
        block_rows, block_grads = pair
        term = jnp.dot(block_rows.T, block_grads, preferred_element_type=jnp.float32)
        return (total + term, None)
    total, unused = lax.scan(add_block, jnp.zeros((D, KW), jnp.float32), (scaled_blocks, grad_blocks))
    weight_grads = total / groups
    return (input_grads, weight_grads, gain_grads)
```

```python
import functools

import jax
import jax.numpy as jnp
from jax import lax
from jax.experimental import pallas as pl
from jax.experimental.pallas import tpu as pltpu
from jax.sharding import PartitionSpec as P

AXES = ("grp", "sub")
EPS = 1e-05
F32 = jnp.float32
BF16 = jnp.bfloat16
VMEM_LIMIT = 48 * 1024 * 1024


def params():
    return pltpu.CompilerParams(vmem_limit_bytes=VMEM_LIMIT)


class Plan:
    def __init__(self, groups, subs):
        self.groups, self.subs = groups, subs
        self.width = groups // 2
        self.depth = subs // self.width

    def index(self, core, y, x, z):
        return (y * 2 + core) * self.subs + z * self.width + x

    def pairs(self, move):
        found = []
        for core in range(2):
            for y in range(self.width):
                for x in range(self.width):
                    for z in range(self.depth):
                        found.append((self.index(core, y, x, z), self.index(*move(core, y, x, z))))
        return found

    def send(self, array, move):
        return lax.ppermute(array, AXES, self.pairs(move))


def place(plan):
    grp, sub = lax.axis_index("grp"), lax.axis_index("sub")
    return grp % 2, grp // 2, sub % plan.width, sub // plan.width


def scale_rows(inputs, norm_gain):
    inverse_rms = lax.rsqrt(jnp.mean(inputs * inputs, axis=1, keepdims=True) + EPS)
    return inputs * inverse_rms, inverse_rms


def term_kernel(
    plan, where, acts_ref, peer_acts_ref, gain_ref, grads_ref, peer_grads_ref,
    sent_ref, kept_ref, total,
):
    core, y, x = where[0], where[1], where[2]
    first = jnp.where(core == 0, y, x)
    width, depth = plan.width, plan.depth
    rows = grads_ref.shape[1] // plan.groups
    cols = acts_ref.shape[1] // plan.subs
    gain = gain_ref[...]

    def chosen(ref):
        both = [
            jnp.concatenate(
                [ref[:, (2 * part + half) * rows : (2 * part + half + 1) * rows] for part in range(width)],
                axis=1,
            )
            for half in range(2)
        ]
        return jnp.where(core == 0, both[0].astype(F32), both[1].astype(F32)).astype(BF16)

    for step, (acts, grads) in enumerate(((acts_ref, grads_ref), (peer_acts_ref, peer_grads_ref))):
        normed, _ = scale_rows(acts[...].astype(F32), gain)
        scaled = (normed * gain).astype(BF16)
        term = lax.dot_general(
            chosen(grads), scaled, (((0,), (0,)), ((), ())), preferred_element_type=F32
        )
        if step == 0:
            total[...] = term
        else:
            total[...] += term

    for to_y in range(width):
        for to_x in range(width):
            to_first = jnp.where(core == 0, to_y, to_x)
            to_second = jnp.where(core == 0, to_x, to_y)
            for to_z in range(depth):
                column = (to_z * width + to_x) * cols
                block = total[to_y * rows : (to_y + 1) * rows, column : column + cols]
                slot = to_second * depth + to_z

                @pl.when(to_first == first)
                def _():
                    kept_ref[pl.ds(slot, 1)] = block[None]

                @pl.when(to_first != first)
                def _():
                    sent_ref[pl.ds(slot, 1)] = block.astype(BF16)[None]


def half_kernel(plan, where, kept_ref, got_ref, sent_ref, held_ref):
    core, y, x = where[0], where[1], where[2]
    second = jnp.where(core == 0, x, y)
    depth = plan.depth
    for to_z in range(depth):
        mine = pl.ds(second * depth + to_z, 1)
        other = pl.ds((1 - second) * depth + to_z, 1)
        held_ref[to_z] = (kept_ref[mine] + got_ref[mine].astype(F32))[0]
        sent_ref[to_z] = (kept_ref[other] + got_ref[other].astype(F32))[0].astype(BF16)


def plane_kernel(plan, where, kept_ref, got_ref, held_ref, *sent_refs):
    z = where[3]
    for step in range(plan.depth):
        plane = pl.ds(z ^ step, 1)
        block = (kept_ref[plane] + got_ref[plane].astype(F32))[0]
        if step == 0:
            held_ref[...] = block
        else:
            sent_refs[step - 1][...] = block.astype(BF16)


def last_kernel(plan, held_ref, *refs):
    total = held_ref[...]
    for ref in refs[:-1]:
        total = total + ref[...].astype(F32)
    refs[-1][...] = total.T / plan.groups


def grad_kernel(plan, where, acts_ref, gain_ref, grads_ref, *refs):
    pieces, (out_ref, sums_ref, weight, sems) = refs[:8], refs[8:]
    core, y, x, z = where[0], where[1], where[2], where[3]
    rows = pieces[0].shape[1]
    step = pl.program_id(0)

    @pl.when(step == 0)
    def _():
        copies = []
        for number, piece in enumerate(pieces):
            other_core, other_y, other_x = number // 4, number // 2 % 2, number % 2
            for offset in range(plan.depth):
                sub = (z ^ offset) * plan.width + (x ^ other_x)
                grp = (y ^ other_y) * 2 + (core ^ other_core)
                start = pl.multiple_of((sub * plan.groups + grp) * rows, rows)
                copies.append(
                    pltpu.make_async_copy(
                        piece.at[offset], weight.at[pl.ds(start, rows)], sems.at[number, offset]
                    )
                )
        for copy in copies:
            copy.start()
        for copy in copies:
            copy.wait()
        sums_ref[...] = jnp.zeros_like(sums_ref)

    gain = gain_ref[...]
    normed, inverse_rms = scale_rows(acts_ref[...].astype(F32), gain)
    grad_scaled = lax.dot_general(
        grads_ref[...], weight[...], (((1,), (1,)), ((), ())), preferred_element_type=F32
    )
    sums_ref[...] += jnp.sum(grad_scaled * normed, axis=0, keepdims=True)
    gained = gain * grad_scaled
    mean = jnp.mean(gained * normed, axis=1, keepdims=True)
    out_ref[...] = (inverse_rms * (gained - normed * mean)).astype(BF16)


SMEM = pl.BlockSpec(memory_space=pltpu.SMEM)
VMEM = pl.BlockSpec(memory_space=pltpu.VMEM)


def by_permutes(plan, activations, norm_gain, key_weight, key_grads):
    tokens, model = activations.shape
    key_width = key_grads.shape[1]
    rows, cols = key_width // plan.groups, model // plan.subs
    width, depth = plan.width, plan.depth
    gain = norm_gain.reshape(1, model)
    core, y, x, z = place(plan)
    where = jnp.stack([core, y, x, z]).astype(jnp.int32)
    shape = jax.ShapeDtypeStruct

    def to_core(core, y, x, z):
        return 1 - core, y, x, z

    def to_x(core, y, x, z):
        return core, y, x ^ 1, z

    def to_y(core, y, x, z):
        return core, y ^ 1, x, z

    def to_z(step):
        return lambda core, y, x, z: (core, y, x, z ^ step)

    def y_then(core, y, x, z):
        return (core, y ^ 1, x, z) if core == 0 else (core, y, x ^ 1, z)

    def x_then(core, y, x, z):
        return (core, y, x ^ 1, z) if core == 0 else (core, y ^ 1, x, z)

    peer_acts = plan.send(activations, to_core)
    peer_grads = plan.send(key_grads, to_core)

    piece_rows = cols // plan.groups
    piece = lax.dynamic_slice_in_dim(key_weight, (y * 2 + core) * piece_rows, piece_rows)
    own = jnp.stack([piece] + [plan.send(piece, to_z(step)) for step in range(1, depth)])
    over_x = plan.send(own, to_x)
    over_y = plan.send(own, to_y)
    over_both = plan.send(jnp.where(core == 0, over_x, over_y), y_then)
    side = [own, over_x, over_y, over_both]
    pieces = side + [plan.send(array, to_core) for array in side]

    term = pl.pallas_call(
        functools.partial(term_kernel, plan),
        out_shape=(
            shape((width * depth, rows, cols), BF16),
            shape((width * depth, rows, cols), F32),
        ),
        in_specs=[SMEM] + [VMEM] * 5,
        out_specs=(VMEM, VMEM),
        scratch_shapes=[pltpu.VMEM((width * rows, model), F32)],
        compiler_params=params(),
        name="term",
    )
    sent, kept = term(where, activations, peer_acts, gain, key_grads, peer_grads)
    got = plan.send(sent, y_then)
    sent, kept = pl.pallas_call(
        functools.partial(half_kernel, plan),
        out_shape=(shape((depth, rows, cols), BF16), shape((depth, rows, cols), F32)),
        in_specs=[SMEM, VMEM, VMEM],
        out_specs=(VMEM, VMEM),
        compiler_params=params(),
        name="half",
    )(where, kept, got)
    got = plan.send(sent, x_then)
    held, *sents = pl.pallas_call(
        functools.partial(plane_kernel, plan),
        out_shape=[shape((rows, cols), F32)] + [shape((rows, cols), BF16)] * (depth - 1),
        in_specs=[SMEM, VMEM, VMEM],
        out_specs=[VMEM] * depth,
        compiler_params=params(),
        name="plane",
    )(where, kept, got)
    gots = [plan.send(array, to_z(step + 1)) for step, array in enumerate(sents)]
    weight_grads = pl.pallas_call(
        functools.partial(last_kernel, plan),
        out_shape=shape((cols, rows), F32),
        in_specs=[VMEM] * depth,
        out_specs=VMEM,
        compiler_params=params(),
        name="last",
    )(held, *gots)

    tile = min(tokens, 128)
    input_grads, sums = pl.pallas_call(
        functools.partial(grad_kernel, plan),
        grid=(tokens // tile,),
        out_shape=(shape((tokens, model), BF16), shape((1, model), F32)),
        in_specs=[
            SMEM,
            pl.BlockSpec((tile, model), lambda i: (i, 0)),
            pl.BlockSpec((1, model), lambda i: (0, 0)),
            pl.BlockSpec((tile, key_width), lambda i: (i, 0)),
        ]
        + [pl.BlockSpec(memory_space=pl.ANY)] * 8,
        out_specs=(
            pl.BlockSpec((tile, model), lambda i: (i, 0)),
            pl.BlockSpec((1, model), lambda i: (0, 0)),
        ),
        scratch_shapes=[
            pltpu.VMEM((model, key_width), BF16),
            pltpu.SemaphoreType.DMA((8, depth)),
        ],
        compiler_params=params(),
        name="grad",
    )(where, activations, gain, key_grads, *pieces)

    sums = sums.reshape(depth, width, cols)
    sums = sums + plan.send(sums, to_core)
    sums = sums + plan.send(sums, to_y)
    mine = lax.dynamic_index_in_dim(sums, x, 1, keepdims=False)
    other = lax.dynamic_index_in_dim(sums, 1 - x, 1, keepdims=False)
    sums = mine + plan.send(other, to_x)
    total = lax.dynamic_index_in_dim(sums, z, 0, keepdims=False)
    for step in range(1, depth):
        part = lax.dynamic_index_in_dim(sums, z ^ step, 0, keepdims=False)
        total = total + plan.send(part, to_z(step))
    return input_grads, weight_grads, total / plan.groups


def by_collectives(activations, norm_gain, key_weight, key_grads):
    inputs = activations.astype(F32)
    inverse_rms = lax.rsqrt(jnp.mean(inputs * inputs, axis=1, keepdims=True) + EPS)
    normed = inputs * inverse_rms
    scaled = (normed * norm_gain).astype(BF16)
    grad_scaled = lax.dot_general(
        key_grads,
        lax.all_gather(key_weight, "sub", axis=0, tiled=True),
        (((1,), (1,)), ((), ())),
        preferred_element_type=F32,
    )
    gained = norm_gain * grad_scaled
    input_grads = (
        inverse_rms * (gained - normed * jnp.mean(gained * normed, axis=1, keepdims=True))
    ).astype(BF16)
    groups = lax.axis_size("grp")
    cols = key_weight.shape[0]
    rows = key_grads.shape[1] // groups
    term = lax.dot_general(
        key_grads, scaled, (((0,), (0,)), ((), ())), preferred_element_type=F32
    )
    received = lax.all_to_all(term, "grp", split_axis=0, concat_axis=1, tiled=True)
    shared = jnp.sum(received.reshape(rows, groups, scaled.shape[1]), axis=1)
    owned = lax.psum_scatter(shared, "sub", scatter_dimension=1, tiled=True).T
    summed = lax.psum(jnp.sum(grad_scaled * normed, axis=0), AXES)
    gain_sum = lax.dynamic_slice_in_dim(summed, lax.axis_index("sub") * cols, cols)
    return input_grads, owned / groups, gain_sum / groups


def local(groups, subs, activations, norm_gain, key_weight, key_grads):
    cols = key_weight.shape[0]
    rows = key_grads.shape[1] // groups
    if groups == 4 and subs % 2 == 0 and subs & (subs - 1) == 0 and cols % 128 == 0 and rows % 16 == 0:
        plan = Plan(groups, subs)
        return by_permutes(plan, activations, norm_gain, key_weight, key_grads)
    return by_collectives(activations, norm_gain, key_weight, key_grads)


def solution(mesh):
    return jax.shard_map(
        functools.partial(local, mesh.shape["grp"], mesh.shape["sub"]),
        mesh=mesh,
        in_specs=(P(AXES, None), P(), P("sub", None), P(AXES, None)),
        out_specs=(P(AXES, None), P("sub", "grp"), P("sub")),
        check_vma=False,
    )
```

```python
import functools

import jax
import jax.numpy as jnp
from jax import lax
from jax.experimental import pallas as pl
from jax.experimental.pallas import tpu as pltpu
from jax.sharding import PartitionSpec as P

AXES = ("grp", "sub")
EPS = 1e-05
F32 = jnp.float32
BF16 = jnp.bfloat16
MIB = 1024 * 1024
TILE = 16
CHUNKS = 4


def params(limit):
    return pltpu.CompilerParams(vmem_limit_bytes=limit * MIB)


def cost(flops, moved):
    return pl.CostEstimate(flops=flops, bytes_accessed=moved, transcendentals=0)


class Plan:
    def __init__(self, groups, subs):
        self.groups, self.subs = groups, subs
        self.width = groups // 2
        self.depth = subs // self.width

    def index(self, core, y, x, z):
        return (y * 2 + core) * self.subs + z * self.width + x

    def pairs(self, move):
        found = []
        for core in range(2):
            for y in range(self.width):
                for x in range(self.width):
                    for z in range(self.depth):
                        found.append((self.index(core, y, x, z), self.index(*move(core, y, x, z))))
        return found

    def send(self, array, move):
        return lax.ppermute(array, AXES, self.pairs(move))


def place(plan):
    grp, sub = lax.axis_index("grp"), lax.axis_index("sub")
    return grp % 2, grp // 2, sub % plan.width, sub // plan.width


def slot_of(plan, where, first, second, to_z):
    core = where[0]
    to_x = jnp.where(core == 0, second, first)
    to_y = jnp.where(core == 0, first, second)
    return (to_x * plan.depth + to_z) * plan.width + to_y


def first_and_second(where):
    core, y, x = where[0], where[1], where[2]
    return jnp.where(core == 0, y, x), jnp.where(core == 0, x, y)


def term_kernel(
    plan, where, acts_ref, peer_acts_ref, gain_hbm, grads_ref, peer_grads_ref,
    sent_ref, totals_ref, inverse_ref, acts, grads, gain_ref, scaled, chosen, totals, sems, ends,
):
    core = where[0]
    width, depth = plan.width, plan.depth
    tokens, model = acts.shape[1:]
    rows = grads.shape[1] // plan.groups
    cols = model // plan.subs
    chunk = tokens // CHUNKS

    def fetch(source, target, sem):
        copy = pltpu.make_async_copy(source, target, sem)
        copy.start()
        return copy

    gain_load = fetch(gain_hbm, gain_ref, ends.at[0])
    parts = [pl.ds(part * chunk, chunk) for part in range(CHUNKS)]
    loads = [
        [fetch(source.at[part], acts.at[owner, part], sems.at[owner, k]) for k, part in enumerate(parts)]
        for owner, source in enumerate((acts_ref, peer_acts_ref))
    ]
    grads_load = fetch(grads_ref, grads, ends.at[1])

    def scale(source, first_row, many, base, keep):
        @pl.loop(0, many // TILE, unroll=8)
        def _(step):
            start = pl.multiple_of(first_row + step * TILE, TILE)
            inputs = source[pl.ds(start, TILE), :].astype(F32)
            inverse_rms = lax.rsqrt(jnp.mean(inputs * inputs, axis=1, keepdims=True) + EPS)
            scaled[pl.ds(base + start, TILE), :] = (inputs * inverse_rms * gain_ref[...]).astype(BF16)
            if keep:
                inverse_ref[pl.ds(start, TILE), :] = jnp.broadcast_to(inverse_rms, (TILE, 128))

    def choose(source, base):
        for half in range(2):

            @pl.when(core == half)
            def _():
                for part in range(width):
                    column = (2 * part + half) * rows
                    chosen[part * rows : (part + 1) * rows, base : base + tokens] = source[
                        :, column : column + rows
                    ].T

    choose(peer_grads_ref, tokens)
    gain_load.wait()
    for owner in range(2):
        for part in range(CHUNKS):
            loads[owner][part].wait()
            scale(acts.at[owner], part * chunk, chunk, owner * tokens, owner == 0)
    grads_load.wait()
    choose(grads, 0)

    stores = []
    for to_x in range(width):
        for to_z in range(depth):
            column = (to_z * width + to_x) * cols
            total = jnp.dot(
                chosen[...], scaled[:, column : column + cols], preferred_element_type=F32
            )
            slot = (to_x * depth + to_z) * width
            for to_y in range(width):
                totals[slot + to_y] = total[to_y * rows : (to_y + 1) * rows]
            here = pl.ds(slot, width)
            stores.append(fetch(totals.at[here], totals_ref.at[here], ends.at[2 + slot // width]))

    first, _ = first_and_second(where)
    for second in range(width):
        for to_z in range(depth):
            slot = slot_of(plan, where, 1 - first, second, to_z)
            sent_ref[second * depth + to_z] = totals[pl.ds(slot, 1)][0].astype(BF16)
    for store in stores:
        store.wait()


def load_kept(plan, where, totals_ref, second, kept, sems):
    first, _ = first_and_second(where)
    copies = []
    for to_z in range(plan.depth):
        slot = slot_of(plan, where, first, second, to_z)
        copies.append(pltpu.make_async_copy(totals_ref.at[slot], kept.at[to_z], sems.at[to_z]))
        copies[-1].start()
    for copy in copies:
        copy.wait()


def half_kernel(plan, where, totals_ref, got_ref, sent_ref, kept, sems):
    _, second = first_and_second(where)
    load_kept(plan, where, totals_ref, 1 - second, kept, sems)
    for to_z in range(plan.depth):
        block = kept[to_z] + got_ref[pl.ds((1 - second) * plan.depth + to_z, 1)][0].astype(F32)
        sent_ref[to_z] = block.astype(BF16)


def plane_kernel(plan, where, totals_ref, got_ref, again_ref, held_ref, *refs):
    sent_refs, (kept, sems) = refs[:-2], refs[-2:]
    _, second = first_and_second(where)
    load_kept(plan, where, totals_ref, second, kept, sems)
    for step in range(plan.depth):
        plane = where[3] ^ step
        block = kept[pl.ds(plane, 1)] + got_ref[pl.ds(second * plan.depth + plane, 1)].astype(F32)
        block = (block + again_ref[pl.ds(plane, 1)].astype(F32))[0]
        if step == 0:
            held_ref[...] = block
        else:
            sent_refs[step - 1][...] = block.astype(BF16)


def last_kernel(plan, held_ref, *refs):
    total = held_ref[...]
    for ref in refs[:-1]:
        total = total + ref[...].astype(F32)
    refs[-1][...] = total / plan.groups


def columns(plan, where, flip, step, cols):
    sub = (where[3] ^ step) * plan.width + (where[2] ^ flip)
    return pl.ds(pl.multiple_of(sub * cols, cols), cols)


def load_columns(plan, where, flip, source, target, sems):
    cols = target.shape[-1]
    copies = []
    for step in range(plan.depth):
        here = columns(plan, where, flip, step, cols)
        copies.append(
            pltpu.make_async_copy(source.at[:, here], target.at[step], sems.at[step])
        )
        copies[-1].start()
    return copies


def multiply(plan, where, flip, pieces, acts, gain_ref, grads, inverse, weight, grad_scaled, sums, step):
    core, y = where[0], where[1]
    rows = pieces[0].shape[1]
    tokens, cols = acts.shape[1:]
    for number, piece in enumerate(pieces):
        grp = (y ^ (number % 2)) * 2 + (core ^ (number // 2))
        weight[step, pl.ds(pl.multiple_of(grp * rows, rows), rows)] = piece[step]
    grad_scaled[step] = lax.dot_general(
        grads[...], weight[step], (((1,), (1,)), ((), ())), preferred_element_type=F32
    )
    gain = gain_ref[:, columns(plan, where, flip, step, cols)]
    means = []
    for start in range(0, tokens, TILE):
        part = slice(start, start + TILE)
        scale = inverse[part, :]
        mean = None
        for lane in range(0, cols, 128):
            lanes = slice(lane, lane + 128)
            product = grad_scaled[step, part, lanes] * (acts[step, part, lanes].astype(F32) * scale)
            total = product[:8] + product[8:]
            if start == 0:
                sums[8 * step : 8 * step + 8, lanes] = total
            else:
                sums[8 * step : 8 * step + 8, lanes] += total
            product = product * gain[:, lanes]
            mean = product if mean is None else mean + product
        means.append((part, mean))
    return means


def finish_sums(plan, sums, sums_ref):
    for step in range(plan.depth):
        sums_ref[step : step + 1, :] = jnp.sum(sums[8 * step : 8 * step + 8, :], axis=0, keepdims=True)


def load_kernel(plan, where, acts_ref, grads_ref, acts, grads, sems):
    load = pltpu.make_async_copy(grads_ref, grads, sems.at[2, 0])
    load.start()
    copies = load_columns(plan, where, 0, acts_ref, acts.at[0], sems.at[0])
    copies += load_columns(plan, where, 1, acts_ref, acts.at[1], sems.at[1])
    load.wait()
    for copy in copies:
        copy.wait()


def near_kernel(plan, where, acts, gain_ref, grads, inverse, *refs):
    pieces, (grad_scaled, mean_ref, sums_ref, weight, sums) = refs[:4], refs[4:]
    for step in range(plan.depth):
        means = multiply(
            plan, where, 0, pieces, acts.at[0], gain_ref, grads, inverse, weight, grad_scaled, sums, step
        )
        for part, mean in means:
            if step == 0:
                mean_ref[part, :] = mean
            else:
                mean_ref[part, :] += mean
    finish_sums(plan, sums, sums_ref)


def far_kernel(plan, where, acts, gain_ref, grads, inverse, near, near_mean, *refs):
    pieces, refs = refs[:4], refs[4:]
    out_ref, sums_ref, weight, grad_scaled, mean_ref, out, sums, ends = refs
    tokens, cols = acts.shape[2:]
    model = cols * plan.subs
    for step in range(plan.depth):
        means = multiply(
            plan, where, 1, pieces, acts.at[1], gain_ref, grads, inverse, weight, grad_scaled, sums, step
        )
        for part, mean in means:
            if step == 0:
                mean_ref[part, :] = near_mean[part, :] + mean
            else:
                mean_ref[part, :] += mean
    finish_sums(plan, sums, sums_ref)
    mean = jnp.sum(mean_ref[...], axis=1, keepdims=True) / model
    mean_ref[...] = jnp.broadcast_to(mean, mean_ref.shape)

    stores = []
    for flip, product in ((1, grad_scaled), (0, near)):
        for step in range(plan.depth):
            here = columns(plan, where, flip, step, cols)
            gain = gain_ref[:, here]
            for start in range(0, tokens, TILE):
                part = slice(start, start + TILE)
                scale = inverse[part, :]
                mean = mean_ref[part, :]
                for lane in range(0, cols, 128):
                    lanes = slice(lane, lane + 128)
                    normed = acts[flip, step, part, lanes].astype(F32) * scale
                    gained = gain[:, lanes] * product[step, part, lanes]
                    out[flip, step, part, lanes] = (scale * (gained - normed * mean)).astype(BF16)
            store = pltpu.make_async_copy(
                out.at[flip, step], out_ref.at[:, here], ends.at[flip * plan.depth + step]
            )
            store.start()
            stores.append(store)
    for store in stores:
        store.wait()


SMEM = pl.BlockSpec(memory_space=pltpu.SMEM)
VMEM = pl.BlockSpec(memory_space=pltpu.VMEM)
HBM = pl.BlockSpec(memory_space=pltpu.HBM)


def by_permutes(plan, activations, norm_gain, key_weight, key_grads):
    tokens, model = activations.shape
    key_width = key_grads.shape[1]
    rows, cols = key_width // plan.groups, model // plan.subs
    width, depth = plan.width, plan.depth
    gain = norm_gain.reshape(1, model)
    core, y, x, z = place(plan)
    where = jnp.stack([core, y, x, z]).astype(jnp.int32)
    shape = jax.ShapeDtypeStruct

    def to_core(core, y, x, z):
        return 1 - core, y, x, z

    def to_x(core, y, x, z):
        return core, y, x ^ 1, z

    def to_y(core, y, x, z):
        return core, y ^ 1, x, z

    def to_xy(core, y, x, z):
        return core, y ^ 1, x ^ 1, z

    def to_z(step):
        return lambda core, y, x, z: (core, y, x, z ^ step)

    def y_then(core, y, x, z):
        return (core, y ^ 1, x, z) if core == 0 else (core, y, x ^ 1, z)

    def x_then(core, y, x, z):
        return (core, y, x ^ 1, z) if core == 0 else (core, y ^ 1, x, z)

    peer_acts = plan.send(activations, to_core)
    peer_grads = plan.send(key_grads, to_core)

    piece_rows = cols // plan.groups
    piece = lax.dynamic_slice_in_dim(key_weight, (y * 2 + core) * piece_rows, piece_rows)
    planes = [plan.send(piece, to_z(step)) for step in range(1, depth)]

    def in_hbm(array):
        return pltpu.with_memory_space_constraint(array, pltpu.HBM)

    acts_hbm, grads_hbm, gain_hbm = in_hbm(activations), in_hbm(key_grads), in_hbm(gain)
    sent, kept, inverse = pl.pallas_call(
        functools.partial(term_kernel, plan),
        out_shape=(
            pltpu.VMEM((width * depth, rows, cols), BF16),
            pltpu.HBM((2 * width * depth, rows, cols), F32),
            pltpu.VMEM((tokens, 128), F32),
        ),
        in_specs=[SMEM, HBM, HBM, HBM, HBM, VMEM],
        out_specs=(VMEM, HBM, VMEM),
        scratch_shapes=[
            pltpu.VMEM((2, tokens, model), BF16),
            pltpu.VMEM((tokens, key_width), BF16),
            pltpu.VMEM((1, model), F32),
            pltpu.VMEM((2 * tokens, model), BF16),
            pltpu.VMEM((width * rows, 2 * tokens), BF16),
            pltpu.VMEM((2 * width * depth, rows, cols), F32),
            pltpu.SemaphoreType.DMA((2, CHUNKS)),
            pltpu.SemaphoreType.DMA((2 + width * depth,)),
        ],
        compiler_params=params(20),
        cost_estimate=cost(4 * tokens * model * width * rows, 20 * MIB),
        name="term",
    )(where, acts_hbm, in_hbm(peer_acts), gain_hbm, grads_hbm, peer_grads)
    got = plan.send(sent, y_then)
    planes, _ = lax.optimization_barrier((planes, sent))
    own = jnp.stack([piece] + planes)
    over_x = plan.send(own, to_x)
    over_y = plan.send(own, to_y)
    over_both = plan.send(jnp.where(core == 0, over_x, over_y), y_then)
    peer_own, peer_over_x, peer_over_y = (
        plan.send(array, to_core) for array in (own, over_x, over_y)
    )
    acts, grads = pl.pallas_call(
        functools.partial(load_kernel, plan),
        out_shape=(
            pltpu.VMEM((2, depth, tokens, cols), BF16),
            pltpu.VMEM((tokens, key_width), BF16),
        ),
        in_specs=[SMEM, HBM, HBM],
        out_specs=[VMEM] * 2,
        scratch_shapes=[pltpu.SemaphoreType.DMA((3, depth))],
        compiler_params=params(1),
        cost_estimate=cost(0, 8 * MIB),
        name="load",
    )(where, acts_hbm, grads_hbm)
    (acts, grads), _ = lax.optimization_barrier(((acts, grads), own))
    over_y, _ = lax.optimization_barrier((over_y, acts))
    near, near_mean, near_sums = pl.pallas_call(
        functools.partial(near_kernel, plan),
        out_shape=(
            shape((depth, tokens, cols), F32),
            shape((tokens, 128), F32),
            shape((depth, cols), F32),
        ),
        in_specs=[SMEM] + [VMEM] * 8,
        out_specs=[VMEM] * 3,
        scratch_shapes=[
            pltpu.VMEM((depth, cols, key_width), BF16),
            pltpu.VMEM((8 * depth, cols), F32),
        ],
        compiler_params=params(6),
        cost_estimate=cost(tokens * model * key_width, 8 * MIB),
        name="near",
    )(where, acts, gain, grads, inverse, own, over_y, peer_own, peer_over_y)
    got, _ = lax.optimization_barrier((got, near))
    kept = in_hbm(kept)
    held_scratch = [pltpu.VMEM((depth, rows, cols), F32), pltpu.SemaphoreType.DMA((depth,))]
    sent = pl.pallas_call(
        functools.partial(half_kernel, plan),
        out_shape=shape((depth, rows, cols), BF16),
        in_specs=[SMEM, HBM, VMEM],
        out_specs=VMEM,
        scratch_shapes=held_scratch,
        compiler_params=params(4),
        cost_estimate=cost(0, 2 * MIB),
        name="half",
    )(where, kept, got)
    near_sums = near_sums + plan.send(near_sums, to_y)
    over_both, near, near_sums, _ = lax.optimization_barrier((over_both, near, near_sums, sent))
    peer_over_both = plan.send(over_both, to_core)
    input_grads, far_sums = pl.pallas_call(
        functools.partial(far_kernel, plan),
        out_shape=(shape((tokens, model), BF16), shape((depth, cols), F32)),
        in_specs=[SMEM] + [VMEM] * 10,
        out_specs=(HBM, VMEM),
        scratch_shapes=[
            pltpu.VMEM((depth, cols, key_width), BF16),
            pltpu.VMEM((depth, tokens, cols), F32),
            pltpu.VMEM((tokens, 128), F32),
            pltpu.VMEM((2, depth, tokens, cols), BF16),
            pltpu.VMEM((8 * depth, cols), F32),
            pltpu.SemaphoreType.DMA((2 * depth,)),
        ],
        compiler_params=params(12),
        cost_estimate=cost(tokens * model * key_width, 8 * MIB),
        name="far",
    )(
        where, acts, gain, grads, inverse, near, near_mean,
        over_x, over_both, peer_over_x, peer_over_both,
    )

    again = plan.send(sent, x_then)
    held, *sents = pl.pallas_call(
        functools.partial(plane_kernel, plan),
        out_shape=[shape((rows, cols), F32)] + [shape((rows, cols), BF16)] * (depth - 1),
        in_specs=[SMEM, HBM, VMEM, VMEM],
        out_specs=[VMEM] * depth,
        scratch_shapes=held_scratch,
        compiler_params=params(4),
        cost_estimate=cost(0, 2 * MIB),
        name="plane",
    )(where, kept, got, again)
    gots = [plan.send(array, to_z(step + 1)) for step, array in enumerate(sents)]
    weight_grads = pl.pallas_call(
        functools.partial(last_kernel, plan),
        out_shape=shape((rows, cols), F32),
        in_specs=[VMEM] * depth,
        out_specs=VMEM,
        compiler_params=params(8),
        cost_estimate=cost(0, 2**20),
        name="last",
    )(held, *gots).T

    sums = (plan.send(far_sums, to_x), plan.send(far_sums, to_xy))
    sums, _ = lax.optimization_barrier((sums, sents))
    sums = near_sums + sums[0] + sums[1]
    sums = sums + plan.send(sums, to_core)
    total = sums[0]
    for step in range(1, depth):
        total = total + plan.send(sums[step], to_z(step))
    return input_grads, weight_grads, total / plan.groups


def by_collectives(activations, norm_gain, key_weight, key_grads):
    inputs = activations.astype(F32)
    inverse_rms = lax.rsqrt(jnp.mean(inputs * inputs, axis=1, keepdims=True) + EPS)
    normed = inputs * inverse_rms
    scaled = (normed * norm_gain).astype(BF16)
    grad_scaled = lax.dot_general(
        key_grads,
        lax.all_gather(key_weight, "sub", axis=0, tiled=True),
        (((1,), (1,)), ((), ())),
        preferred_element_type=F32,
    )
    gained = norm_gain * grad_scaled
    input_grads = (
        inverse_rms * (gained - normed * jnp.mean(gained * normed, axis=1, keepdims=True))
    ).astype(BF16)
    groups = lax.axis_size("grp")
    cols = key_weight.shape[0]
    rows = key_grads.shape[1] // groups
    term = lax.dot_general(
        key_grads, scaled, (((0,), (0,)), ((), ())), preferred_element_type=F32
    )
    received = lax.all_to_all(term, "grp", split_axis=0, concat_axis=1, tiled=True)
    shared = jnp.sum(received.reshape(rows, groups, scaled.shape[1]), axis=1)
    owned = lax.psum_scatter(shared, "sub", scatter_dimension=1, tiled=True).T
    summed = lax.psum(jnp.sum(grad_scaled * normed, axis=0), AXES)
    gain_sum = lax.dynamic_slice_in_dim(summed, lax.axis_index("sub") * cols, cols)
    return input_grads, owned / groups, gain_sum / groups


def local(groups, subs, activations, norm_gain, key_weight, key_grads):
    cols = key_weight.shape[0]
    rows = key_grads.shape[1] // groups
    if groups == 4 and subs % 2 == 0 and subs & (subs - 1) == 0 and cols % 128 == 0 and rows % 16 == 0:
        plan = Plan(groups, subs)
        return by_permutes(plan, activations, norm_gain, key_weight, key_grads)
    return by_collectives(activations, norm_gain, key_weight, key_grads)


def solution(mesh):
    return jax.shard_map(
        functools.partial(local, mesh.shape["grp"], mesh.shape["sub"]),
        mesh=mesh,
        in_specs=(P(AXES, None), P(), P("sub", None), P(AXES, None)),
        out_specs=(P(AXES, None), P("sub", "grp"), P("sub")),
        check_vma=False,
    )
```

```python
import functools

import jax
import jax.numpy as jnp
from jax import lax
from jax.experimental import pallas as pl
from jax.experimental.pallas import tpu as pltpu
from jax.sharding import PartitionSpec as P

AXES = ("grp", "sub")
EPS = 1e-05
F32 = jnp.float32
BF16 = jnp.bfloat16
MIB = 1024 * 1024
TILE = 16
CHUNKS = 4


def params(limit):
    return pltpu.CompilerParams(vmem_limit_bytes=limit * MIB)


def cost(flops, moved):
    return pl.CostEstimate(flops=0, bytes_accessed=0, transcendentals=0)


class Plan:
    def __init__(self, groups, subs):
        self.groups, self.subs = groups, subs
        self.width = groups // 2
        self.depth = subs // self.width

    def index(self, core, y, x, z):
        return (y * 2 + core) * self.subs + z * self.width + x

    def pairs(self, move):
        found = []
        for core in range(2):
            for y in range(self.width):
                for x in range(self.width):
                    for z in range(self.depth):
                        found.append((self.index(core, y, x, z), self.index(*move(core, y, x, z))))
        return found

    def send(self, array, move):
        return lax.ppermute(array, AXES, self.pairs(move))


def place(plan):
    grp, sub = lax.axis_index("grp"), lax.axis_index("sub")
    return grp % 2, grp // 2, sub % plan.width, sub // plan.width


def slot_of(plan, where, first, second, to_z):
    core = where[0]
    to_x = jnp.where(core == 0, second, first)
    to_y = jnp.where(core == 0, first, second)
    return (to_x * plan.depth + to_z) * plan.width + to_y


def first_and_second(where):
    core, y, x = where[0], where[1], where[2]
    return jnp.where(core == 0, y, x), jnp.where(core == 0, x, y)


def fetch(source, target, sem):
    copy = pltpu.make_async_copy(source, target, sem)
    copy.start()
    return copy


def fetch_rows(source, target, sems):
    chunk = target.shape[0] // CHUNKS
    parts = [pl.ds(part * chunk, chunk) for part in range(CHUNKS)]
    return [fetch(source.at[part], target.at[part], sems.at[k]) for k, part in enumerate(parts)]


def scale_rows(source, gain, scaled, start, stop):
    @pl.loop(0, (stop - start) // TILE, unroll=8)
    def _(step):
        part = pl.ds(pl.multiple_of(start + step * TILE, TILE), TILE)
        inputs = source[part, :].astype(F32)
        inverse_rms = lax.rsqrt(jnp.mean(inputs * inputs, axis=1, keepdims=True) + EPS)
        scaled[part, :] = (inputs * inverse_rms * gain[...]).astype(BF16)


def mine_kernel(
    plan, where, acts_ref, gain_ref, grads_ref, weight_ref,
    scaled, mine, other, piece, acts, grads, gain, weight, sems, ends,
):
    core = where[0]
    tokens = acts.shape[0]
    rows = grads.shape[1] // plan.groups
    load = fetch(gain_ref, gain, ends.at[0])
    loads = fetch_rows(acts_ref, acts, sems)
    grads_load = fetch(grads_ref, grads, ends.at[1])
    weight_load = fetch(weight_ref, weight, ends.at[2])
    load.wait()
    chunk = tokens // CHUNKS
    for part in range(CHUNKS):
        loads[part].wait()
        scale_rows(acts, gain, scaled, part * chunk, (part + 1) * chunk)
    grads_load.wait()
    for half, (even, odd) in enumerate(((mine, other), (other, mine))):

        @pl.when(core == half)
        def _():
            for part in range(plan.width):
                place = slice(part * rows, (part + 1) * rows)
                column = 2 * part * rows
                even[place, :] = grads[:, column : column + rows].T
                odd[place, :] = grads[:, column + rows : column + 2 * rows].T

    weight_load.wait()
    for number in range(plan.groups):

        @pl.when(where[1] * 2 + core == number)
        def _():
            piece[...] = weight[:, number * rows : (number + 1) * rows].T


def term_kernel(
    plan, where, acts, gain_ref, scaled, mine, theirs,
    sent_ref, kept_ref, held_ref, gain, peer_scaled, totals, end,
):
    width, depth = plan.width, plan.depth
    tokens, model = acts.shape
    rows = mine.shape[0] // width
    cols = model // plan.subs
    fetch(gain_ref, gain, end).wait()
    scale_rows(acts, gain, peer_scaled, 0, tokens)

    for to_x in range(width):
        for to_z in range(depth):
            column = (to_z * width + to_x) * cols
            here = slice(column, column + cols)
            total = jnp.dot(mine[...], scaled[:, here], preferred_element_type=F32)
            total += jnp.dot(theirs[...], peer_scaled[:, here], preferred_element_type=F32)
            slot = (to_x * depth + to_z) * width
            for to_y in range(width):
                totals[slot + to_y] = total[to_y * rows : (to_y + 1) * rows]

    first, mine_second = first_and_second(where)
    for to_z in range(depth):
        for second in range(width):
            slot = slot_of(plan, where, 1 - first, second, to_z)
            sent_ref[second * depth + to_z] = totals[pl.ds(slot, 1)][0].astype(BF16)
        for second, out_ref in ((1 - mine_second, kept_ref), (mine_second, held_ref)):
            out_ref[to_z] = totals[pl.ds(slot_of(plan, where, first, second, to_z), 1)][0]


def half_kernel(plan, where, kept, got_ref, *refs):
    pieces, sent_ref = refs[:-1], refs[-1]
    _, second = first_and_second(where)
    for step, piece in enumerate(pieces):
        sent_ref[plan.depth + step] = piece[...]
    for to_z in range(plan.depth):
        block = kept[to_z] + got_ref[pl.ds((1 - second) * plan.depth + to_z, 1)][0].astype(F32)
        sent_ref[to_z] = block.astype(BF16)


def pack_kernel(plan, sent_ref, late_ref, got_ref, late_got_ref, out_ref):
    depth = plan.depth
    for part, (early, late) in enumerate(((sent_ref, late_ref), (got_ref, late_got_ref))):
        out_ref[part * depth : (part + 1) * depth - 1] = early[depth:]
        out_ref[(part + 1) * depth - 1] = late[...]


def plane_kernel(plan, where, held, got_ref, own, again_ref, gain_ref, sums_ref, gains_ref, *sent_refs):
    _, second = first_and_second(where)
    rows, cols = sums_ref.shape
    for step in range(plan.depth):
        plane = where[3] ^ step
        block = held[pl.ds(plane, 1)] + got_ref[pl.ds(second * plan.depth + plane, 1)].astype(F32)
        block = (block + again_ref[pl.ds(plane, 1)].astype(F32))[0]
        gains = jnp.sum(block * own[step].astype(F32), axis=0, keepdims=True)
        gains = gains / gain_ref[:, columns(plan, where, 0, step, cols)]
        if step == 0:
            sums_ref[...] = block
            gains_ref[...] = gains
        else:
            sent_refs[step - 1][:rows, :] = block.astype(BF16)
            row = lax.broadcasted_iota(jnp.int32, (16, cols), 0)
            tail = jnp.zeros((16, cols), F32)
            for number in range(3):
                high = gains.astype(BF16).astype(F32)
                tail = jnp.where(row == number, high, tail)
                gains = gains - high
            sent_refs[step - 1][rows:, :] = tail.astype(BF16)


def last_kernel(plan, sums_ref, gains_ref, *refs):
    got_refs, (out_ref, out_gains_ref) = refs[:-2], refs[-2:]
    rows = sums_ref.shape[0]
    total, gains = sums_ref[...], gains_ref[...]
    for ref in got_refs:
        total = total + ref[:rows, :].astype(F32)
        gains = gains + jnp.sum(ref[rows:, :].astype(F32), axis=0, keepdims=True)
    out_ref[...] = total / plan.groups
    out_gains_ref[...] = gains


def columns(plan, where, flip, step, cols):
    sub = (where[3] ^ step) * plan.width + (where[2] ^ flip)
    return pl.ds(pl.multiple_of(sub * cols, cols), cols)


def load_kernel(plan, where, acts_ref, grads_ref, acts, grads, inverse, sems):
    load = fetch(grads_ref, grads, sems.at[2, 0])
    cols = acts.shape[-1]
    copies = [
        fetch(acts_ref.at[:, columns(plan, where, flip, step, cols)], acts.at[flip, step], sems.at[flip, step])
        for flip in range(2)
        for step in range(plan.depth)
    ]
    load.wait()
    tokens = grads.shape[0]
    for number, copy in enumerate(copies):
        copy.wait()
        block = acts.at[number // plan.depth, number % plan.depth]
        for start in range(0, tokens, TILE):
            part = slice(start, start + TILE)
            square = None
            for lane in range(0, cols, 128):
                inputs = block[part, lane : lane + 128].astype(F32)
                square = inputs * inputs if square is None else square + inputs * inputs
            if number == 0:
                inverse[part, :] = square
            else:
                inverse[part, :] += square
    mean_square = jnp.sum(inverse[...], axis=1, keepdims=True) / (2 * plan.depth * cols)
    inverse[...] = jnp.broadcast_to(lax.rsqrt(mean_square + EPS), inverse.shape)


def place_weight(plan, where, pieces, from_core, second, weight):
    depth = plan.depth
    rows = pieces.shape[1]
    for part in range(2):
        if second:
            flip = from_core if part == 0 else 1
            far_y = (1 - from_core) if part == 0 else 1
        else:
            flip = 0 if part == 0 else 1 - from_core
            far_y = 0 if part == 0 else from_core
        grp = (where[1] ^ far_y) * 2 + from_core
        here = pl.ds(pl.multiple_of(grp * rows, rows), rows)
        for step in range(depth):
            weight[pl.ds(flip * depth + step, 1), here] = pieces[part * depth + step][None]


def grad_kernel(
    plan, where, acts, gain_ref, grads, inverse, mine_sent, mine_got, peer_sent, peer_got,
    out_ref, weight, grad_scaled, mean_ref, out, ends,
):
    core = where[0]
    depth = plan.depth
    tokens, cols = acts.shape[2:]
    model = cols * plan.subs
    place_weight(plan, where, mine_sent, core, False, weight)
    place_weight(plan, where, peer_sent, 1 - core, False, weight)
    place_weight(plan, where, mine_got, core, True, weight)
    place_weight(plan, where, peer_got, 1 - core, True, weight)
    blocks = [(flip, step) for flip in range(2) for step in range(depth)]
    for flip, step in blocks:
        number = flip * depth + step
        grad_scaled[number] = jnp.dot(grads[...], weight[number], preferred_element_type=F32)
        gain = gain_ref[:, columns(plan, where, flip, step, cols)]
        for start in range(0, tokens, TILE):
            part = slice(start, start + TILE)
            scale = inverse[part, :]
            mean = None
            for lane in range(0, cols, 128):
                lanes = slice(lane, lane + 128)
                normed = acts[flip, step, part, lanes].astype(F32) * scale
                product = gain[:, lanes] * grad_scaled[number, part, lanes] * normed
                mean = product if mean is None else mean + product
            if number == 0:
                mean_ref[part, :] = mean
            else:
                mean_ref[part, :] += mean
    mean = jnp.sum(mean_ref[...], axis=1, keepdims=True) / model
    mean_ref[...] = jnp.broadcast_to(mean, mean_ref.shape)

    stores = []
    for flip, step in blocks:
        number = flip * depth + step
        here = columns(plan, where, flip, step, cols)
        gain = gain_ref[:, here]
        for start in range(0, tokens, TILE):
            part = slice(start, start + TILE)
            scale = inverse[part, :]
            mean = mean_ref[part, :]
            for lane in range(0, cols, 128):
                lanes = slice(lane, lane + 128)
                normed = acts[flip, step, part, lanes].astype(F32) * scale
                gained = gain[:, lanes] * grad_scaled[number, part, lanes]
                out[number, part, lanes] = (scale * (gained - normed * mean)).astype(BF16)
        stores.append(fetch(out.at[number], out_ref.at[:, here], ends.at[number]))
    for store in stores:
        store.wait()


SMEM = pl.BlockSpec(memory_space=pltpu.SMEM)
VMEM = pl.BlockSpec(memory_space=pltpu.VMEM)
HBM = pl.BlockSpec(memory_space=pltpu.HBM)


def by_permutes(plan, activations, norm_gain, key_weight, key_grads):
    tokens, model = activations.shape
    key_width = key_grads.shape[1]
    rows, cols = key_width // plan.groups, model // plan.subs
    width, depth = plan.width, plan.depth
    gain = norm_gain.reshape(1, model)
    core, y, x, z = place(plan)
    where = jnp.stack([core, y, x, z]).astype(jnp.int32)
    shape = jax.ShapeDtypeStruct

    def to_core(core, y, x, z):
        return 1 - core, y, x, z

    def to_x(core, y, x, z):
        return core, y, x ^ 1, z

    def to_y(core, y, x, z):
        return core, y ^ 1, x, z

    def to_z(step):
        return lambda core, y, x, z: (core, y, x, z ^ step)

    def y_then(core, y, x, z):
        return (core, y ^ 1, x, z) if core == 0 else (core, y, x ^ 1, z)

    def x_then(core, y, x, z):
        return (core, y, x ^ 1, z) if core == 0 else (core, y ^ 1, x, z)

    def in_hbm(array):
        return pltpu.with_memory_space_constraint(array, pltpu.HBM)

    acts_hbm, grads_hbm, gain_hbm = in_hbm(activations), in_hbm(key_grads), in_hbm(gain)

    peer_acts = plan.send(activations, to_core)
    half_shape = (width * rows, tokens)
    scaled, mine, other, piece = pl.pallas_call(
        functools.partial(mine_kernel, plan),
        out_shape=(
            pltpu.VMEM((tokens, model), BF16),
            pltpu.VMEM(half_shape, BF16),
            pltpu.VMEM(half_shape, BF16),
            pltpu.VMEM((rows, cols), BF16),
        ),
        in_specs=[SMEM, HBM, HBM, HBM, HBM],
        out_specs=[VMEM] * 4,
        scratch_shapes=[
            pltpu.VMEM((tokens, model), BF16),
            pltpu.VMEM((tokens, key_width), BF16),
            pltpu.VMEM((1, model), F32),
            pltpu.VMEM((cols, key_width), BF16),
            pltpu.SemaphoreType.DMA((CHUNKS,)),
            pltpu.SemaphoreType.DMA((3,)),
        ],
        compiler_params=params(5),
        cost_estimate=cost(0, 8 * MIB),
        name="mine",
    )(where, acts_hbm, gain_hbm, grads_hbm, in_hbm(key_weight))
    theirs = plan.send(other, to_core)
    sent, kept, held = pl.pallas_call(
        functools.partial(term_kernel, plan),
        out_shape=(
            pltpu.VMEM((width * depth, rows, cols), BF16),
            pltpu.VMEM((depth, rows, cols), F32),
            pltpu.VMEM((depth, rows, cols), F32),
        ),
        in_specs=[SMEM, VMEM, HBM, VMEM, VMEM, VMEM],
        out_specs=[VMEM] * 3,
        scratch_shapes=[
            pltpu.VMEM((1, model), F32),
            pltpu.VMEM((tokens, model), BF16),
            pltpu.VMEM((2 * width * depth, rows, cols), F32),
            pltpu.SemaphoreType.DMA(()),
        ],
        compiler_params=params(8),
        cost_estimate=cost(4 * tokens * model * width * rows, 20 * MIB),
        name="term",
    )(where, peer_acts, gain_hbm, scaled, mine, theirs)
    got = plan.send(sent, y_then)

    acts, grads, inverse = pl.pallas_call(
        functools.partial(load_kernel, plan),
        out_shape=(
            pltpu.VMEM((2, depth, tokens, cols), BF16),
            pltpu.VMEM((tokens, key_width), BF16),
            pltpu.VMEM((tokens, 128), F32),
        ),
        in_specs=[SMEM, HBM, HBM],
        out_specs=[VMEM] * 3,
        scratch_shapes=[pltpu.SemaphoreType.DMA((3, depth))],
        compiler_params=params(1),
        cost_estimate=cost(0, 8 * MIB),
        name="load",
    )(where, acts_hbm, grads_hbm)

    pieces = [piece] + [plan.send(piece, to_z(step)) for step in range(1, depth - 1)]
    got, pieces, acts, grads = lax.optimization_barrier((got, pieces, acts, grads))

    both = (2 * depth, rows, cols)
    sent = pl.pallas_call(
        functools.partial(half_kernel, plan),
        out_shape=pltpu.VMEM((2 * depth - 1, rows, cols), BF16),
        in_specs=[SMEM] + [VMEM] * (1 + depth),
        out_specs=VMEM,
        compiler_params=params(2),
        cost_estimate=cost(0, 2 * MIB),
        name="half",
    )(where, kept, got, *pieces)
    again = plan.send(sent, x_then)
    late = plan.send(pieces[0], to_z(depth - 1))
    late_again = plan.send(late, x_then)
    mine_sent = pl.pallas_call(
        functools.partial(pack_kernel, plan),
        out_shape=pltpu.VMEM(both, BF16),
        in_specs=[VMEM] * 4,
        out_specs=VMEM,
        compiler_params=params(1),
        cost_estimate=cost(0, 2 * MIB),
        name="pack",
    )(sent, late, again, late_again)
    mine_got = plan.send(mine_sent, y_then)
    peer_sent = plan.send(mine_sent, to_core)
    sums, gains, *sents = pl.pallas_call(
        functools.partial(plane_kernel, plan),
        out_shape=[pltpu.VMEM((rows, cols), F32), pltpu.VMEM((1, cols), F32)]
        + [pltpu.VMEM((rows + 16, cols), BF16)] * (depth - 1),
        in_specs=[SMEM] + [VMEM] * 5,
        out_specs=[VMEM] * (1 + depth),
        compiler_params=params(3),
        cost_estimate=cost(0, 2 * MIB),
        name="plane",
    )(where, held, got, mine_sent, again, gain)
    gots = [plan.send(array, to_z(step + 1)) for step, array in enumerate(sents)]
    mine_got, gots = lax.optimization_barrier((mine_got, gots))
    peer_got = plan.send(mine_got, to_core)
    weight_grads, gains = pl.pallas_call(
        functools.partial(last_kernel, plan),
        out_shape=(shape((rows, cols), F32), pltpu.VMEM((1, cols), F32)),
        in_specs=[VMEM] * (depth + 1),
        out_specs=(VMEM, VMEM),
        compiler_params=params(2),
        cost_estimate=cost(0, MIB),
        name="last",
    )(sums, gains, *gots)
    gains, peer_got = lax.optimization_barrier((gains, peer_got))
    gains = gains + plan.send(gains, to_core)
    gains = gains + plan.send(gains, to_y)

    input_grads = pl.pallas_call(
        functools.partial(grad_kernel, plan),
        out_shape=shape((tokens, model), BF16),
        in_specs=[SMEM] + [VMEM] * 8,
        out_specs=HBM,
        scratch_shapes=[
            pltpu.VMEM((2 * depth, key_width, cols), BF16),
            pltpu.VMEM((2 * depth, tokens, cols), F32),
            pltpu.VMEM((tokens, 128), F32),
            pltpu.VMEM((2 * depth, tokens, cols), BF16),
            pltpu.SemaphoreType.DMA((2 * depth,)),
        ],
        compiler_params=params(12),
        cost_estimate=cost(2 * tokens * model * key_width, 8 * MIB),
        name="grad",
    )(where, acts, gain, grads, inverse, mine_sent, mine_got, peer_sent, peer_got)
    return input_grads, weight_grads.T, gains.reshape(cols) / plan.groups


def by_collectives(activations, norm_gain, key_weight, key_grads):
    inputs = activations.astype(F32)
    inverse_rms = lax.rsqrt(jnp.mean(inputs * inputs, axis=1, keepdims=True) + EPS)
    normed = inputs * inverse_rms
    scaled = (normed * norm_gain).astype(BF16)
    grad_scaled = lax.dot_general(
        key_grads,
        lax.all_gather(key_weight, "sub", axis=0, tiled=True),
        (((1,), (1,)), ((), ())),
        preferred_element_type=F32,
    )
    gained = norm_gain * grad_scaled
    input_grads = (
        inverse_rms * (gained - normed * jnp.mean(gained * normed, axis=1, keepdims=True))
    ).astype(BF16)
    groups = lax.axis_size("grp")
    cols = key_weight.shape[0]
    rows = key_grads.shape[1] // groups
    term = lax.dot_general(
        key_grads, scaled, (((0,), (0,)), ((), ())), preferred_element_type=F32
    )
    received = lax.all_to_all(term, "grp", split_axis=0, concat_axis=1, tiled=True)
    shared = jnp.sum(received.reshape(rows, groups, scaled.shape[1]), axis=1)
    owned = lax.psum_scatter(shared, "sub", scatter_dimension=1, tiled=True).T
    summed = lax.psum(jnp.sum(grad_scaled * normed, axis=0), AXES)
    gain_sum = lax.dynamic_slice_in_dim(summed, lax.axis_index("sub") * cols, cols)
    return input_grads, owned / groups, gain_sum / groups


def local(groups, subs, activations, norm_gain, key_weight, key_grads):
    cols = key_weight.shape[0]
    rows = key_grads.shape[1] // groups
    if groups == 4 and subs % 2 == 0 and subs & (subs - 1) == 0 and cols % 128 == 0 and rows % 16 == 0:
        plan = Plan(groups, subs)
        return by_permutes(plan, activations, norm_gain, key_weight, key_grads)
    return by_collectives(activations, norm_gain, key_weight, key_grads)


def solution(mesh):
    return jax.shard_map(
        functools.partial(local, mesh.shape["grp"], mesh.shape["sub"]),
        mesh=mesh,
        in_specs=(P(AXES, None), P(), P("sub", None), P(AXES, None)),
        out_specs=(P(AXES, None), P("sub", "grp"), P("sub")),
        check_vma=False,
    )
```

```python
import functools

import jax
import jax.numpy as jnp
from jax import lax
from jax.experimental import pallas as pl
from jax.experimental.pallas import tpu as pltpu
from jax.sharding import PartitionSpec as P

AXES = ("grp", "sub")
EPS = 1e-05
F32 = jnp.float32
BF16 = jnp.bfloat16
MIB = 1024 * 1024
TILE = 16
CHUNKS = 4
EARLY = 1


def params(limit):
    return pltpu.CompilerParams(vmem_limit_bytes=limit * MIB)


def cost(flops, moved):
    return pl.CostEstimate(flops=0, bytes_accessed=0, transcendentals=0)


class Plan:
    def __init__(self, groups, subs):
        self.groups, self.subs = groups, subs
        self.width = groups // 2
        self.depth = subs // self.width

    def index(self, core, y, x, z):
        return (y * 2 + core) * self.subs + z * self.width + x

    def pairs(self, move):
        found = []
        for core in range(2):
            for y in range(self.width):
                for x in range(self.width):
                    for z in range(self.depth):
                        found.append((self.index(core, y, x, z), self.index(*move(core, y, x, z))))
        return found

    def send(self, array, move):
        return lax.ppermute(array, AXES, self.pairs(move))


def place(plan):
    grp, sub = lax.axis_index("grp"), lax.axis_index("sub")
    return grp % 2, grp // 2, sub % plan.width, sub // plan.width


def slot_of(plan, where, first, second, to_z):
    core = where[0]
    to_x = jnp.where(core == 0, second, first)
    to_y = jnp.where(core == 0, first, second)
    return (to_x * plan.depth + to_z) * plan.width + to_y


def first_and_second(where):
    core, y, x = where[0], where[1], where[2]
    return jnp.where(core == 0, y, x), jnp.where(core == 0, x, y)


def fetch(source, target, sem):
    copy = pltpu.make_async_copy(source, target, sem)
    copy.start()
    return copy


def fetch_rows(source, target, sems):
    chunk = target.shape[0] // CHUNKS
    parts = [pl.ds(part * chunk, chunk) for part in range(CHUNKS)]
    return [fetch(source.at[part], target.at[part], sems.at[k]) for k, part in enumerate(parts)]


def scale_rows(source, gain, scaled, start, stop):
    @pl.loop(0, (stop - start) // TILE, unroll=8)
    def _(step):
        part = pl.ds(pl.multiple_of(start + step * TILE, TILE), TILE)
        inputs = source[part, :].astype(F32)
        inverse_rms = lax.rsqrt(jnp.mean(inputs * inputs, axis=1, keepdims=True) + EPS)
        scaled[part, :] = (inputs * inverse_rms * gain[...]).astype(BF16)


def mine_kernel(
    plan, where, acts_ref, gain_ref, grads_ref, weight_ref,
    scaled, mine, other, piece, acts, grads, gain, weight, sems, ends,
):
    core = where[0]
    tokens = acts.shape[0]
    rows = grads.shape[1] // plan.groups
    load = fetch(gain_ref, gain, ends.at[0])
    loads = fetch_rows(acts_ref, acts, sems)
    grads_load = fetch(grads_ref, grads, ends.at[1])
    weight_load = fetch(weight_ref, weight, ends.at[2])
    load.wait()
    chunk = tokens // CHUNKS
    for part in range(CHUNKS):
        loads[part].wait()
        scale_rows(acts, gain, scaled, part * chunk, (part + 1) * chunk)
    grads_load.wait()
    for half, (even, odd) in enumerate(((mine, other), (other, mine))):

        @pl.when(core == half)
        def _():
            for part in range(plan.width):
                place = slice(part * rows, (part + 1) * rows)
                column = 2 * part * rows
                even[place, :] = grads[:, column : column + rows].T
                odd[place, :] = grads[:, column + rows : column + 2 * rows].T

    weight_load.wait()
    for number in range(plan.groups):

        @pl.when(where[1] * 2 + core == number)
        def _():
            piece[...] = weight[:, number * rows : (number + 1) * rows].T


def term_kernel(
    plan, where, acts, gain_ref, scaled, mine, theirs,
    sent_ref, kept_ref, held_ref, gain, peer_scaled, totals, end,
):
    width, depth = plan.width, plan.depth
    tokens, model = acts.shape
    rows = mine.shape[0] // width
    cols = model // plan.subs
    fetch(gain_ref, gain, end).wait()
    scale_rows(acts, gain, peer_scaled, 0, tokens)

    for to_x in range(width):
        for to_z in range(depth):
            column = (to_z * width + to_x) * cols
            here = slice(column, column + cols)
            total = jnp.dot(mine[...], scaled[:, here], preferred_element_type=F32)
            total += jnp.dot(theirs[...], peer_scaled[:, here], preferred_element_type=F32)
            slot = (to_x * depth + to_z) * width
            for to_y in range(width):
                totals[slot + to_y] = total[to_y * rows : (to_y + 1) * rows]

    first, mine_second = first_and_second(where)
    for to_z in range(depth):
        for second in range(width):
            slot = slot_of(plan, where, 1 - first, second, to_z)
            sent_ref[second * depth + to_z] = totals[pl.ds(slot, 1)][0].astype(BF16)
        for second, out_ref in ((1 - mine_second, kept_ref), (mine_second, held_ref)):
            out_ref[to_z] = totals[pl.ds(slot_of(plan, where, first, second, to_z), 1)][0]


def half_kernel(plan, where, kept, got_ref, sent_ref):
    _, second = first_and_second(where)
    for to_z in range(plan.depth):
        block = kept[to_z] + got_ref[pl.ds((1 - second) * plan.depth + to_z, 1)][0].astype(F32)
        sent_ref[to_z] = block.astype(BF16)


def pack_kernel(plan, *refs):
    for number, ref in enumerate(refs[:-1]):
        refs[-1][number] = ref[...]


def plane_kernel(plan, where, held, got_ref, own, again_ref, gain_ref, sums_ref, gains_ref, *sent_refs):
    _, second = first_and_second(where)
    rows, cols = sums_ref.shape
    for step in range(plan.depth):
        plane = where[3] ^ step
        block = held[pl.ds(plane, 1)] + got_ref[pl.ds(second * plan.depth + plane, 1)].astype(F32)
        block = (block + again_ref[pl.ds(plane, 1)].astype(F32))[0]
        gains = jnp.sum(block * own[step].astype(F32), axis=0, keepdims=True)
        gains = gains / gain_ref[:, columns(plan, where, 0, step, cols)]
        if step == 0:
            sums_ref[...] = block
            gains_ref[...] = gains
        else:
            sent_refs[step - 1][:rows, :] = block.astype(BF16)
            row = lax.broadcasted_iota(jnp.int32, (16, cols), 0)
            tail = jnp.zeros((16, cols), F32)
            for number in range(3):
                high = gains.astype(BF16).astype(F32)
                tail = jnp.where(row == number, high, tail)
                gains = gains - high
            sent_refs[step - 1][rows:, :] = tail.astype(BF16)


def last_kernel(plan, sums_ref, gains_ref, *refs):
    got_refs, (out_ref, out_gains_ref) = refs[:-2], refs[-2:]
    rows = sums_ref.shape[0]
    total, gains = sums_ref[...], gains_ref[...]
    for ref in got_refs:
        total = total + ref[:rows, :].astype(F32)
        gains = gains + jnp.sum(ref[rows:, :].astype(F32), axis=0, keepdims=True)
    out_ref[...] = total / plan.groups
    out_gains_ref[...] = gains


def columns(plan, where, flip, step, cols):
    sub = (where[3] ^ step) * plan.width + (where[2] ^ flip)
    return pl.ds(pl.multiple_of(sub * cols, cols), cols)


def load_kernel(plan, where, acts_ref, grads_ref, acts, grads, inverse, sems):
    load = fetch(grads_ref, grads, sems.at[2, 0])
    cols = acts.shape[-1]
    copies = [
        fetch(acts_ref.at[:, columns(plan, where, flip, step, cols)], acts.at[flip, step], sems.at[flip, step])
        for flip in range(2)
        for step in range(plan.depth)
    ]
    load.wait()
    tokens = grads.shape[0]
    for number, copy in enumerate(copies):
        copy.wait()
        block = acts.at[number // plan.depth, number % plan.depth]
        for start in range(0, tokens, TILE):
            part = slice(start, start + TILE)
            square = None
            for lane in range(0, cols, 128):
                inputs = block[part, lane : lane + 128].astype(F32)
                square = inputs * inputs if square is None else square + inputs * inputs
            if number == 0:
                inverse[part, :] = square
            else:
                inverse[part, :] += square
    mean_square = jnp.sum(inverse[...], axis=1, keepdims=True) / (2 * plan.depth * cols)
    inverse[...] = jnp.broadcast_to(lax.rsqrt(mean_square + EPS), inverse.shape)


def place_weight(plan, where, pieces, from_core, second, weight):
    depth = plan.depth
    blocks = [array.at[number] for array in pieces for number in range(array.shape[0])]
    rows = blocks[0].shape[0]
    for part in range(2):
        if second:
            flip = from_core if part == 0 else 1
            far_y = (1 - from_core) if part == 0 else 1
        else:
            flip = 0 if part == 0 else 1 - from_core
            far_y = 0 if part == 0 else from_core
        grp = (where[1] ^ far_y) * 2 + from_core
        here = pl.ds(pl.multiple_of(grp * rows, rows), rows)
        for step in range(depth):
            weight[pl.ds(flip * depth + step, 1), here] = blocks[part * depth + step][...][None]


def grad_kernel(
    plan, where, acts, gain_ref, grads, inverse, mine_sent, mine_got, peer_first, peer_rest, peer_got,
    out_ref, weight, grad_scaled, mean_ref, out, ends,
):
    core = where[0]
    depth = plan.depth
    tokens, cols = acts.shape[2:]
    model = cols * plan.subs
    place_weight(plan, where, [mine_sent], core, False, weight)
    place_weight(plan, where, [peer_first, peer_rest], 1 - core, False, weight)
    place_weight(plan, where, [mine_got], core, True, weight)
    place_weight(plan, where, [peer_got], 1 - core, True, weight)
    blocks = [(flip, step) for flip in range(2) for step in range(depth)]
    for flip, step in blocks:
        number = flip * depth + step
        grad_scaled[number] = jnp.dot(grads[...], weight[number], preferred_element_type=F32)
        gain = gain_ref[:, columns(plan, where, flip, step, cols)]
        for start in range(0, tokens, TILE):
            part = slice(start, start + TILE)
            scale = inverse[part, :]
            mean = None
            for lane in range(0, cols, 128):
                lanes = slice(lane, lane + 128)
                normed = acts[flip, step, part, lanes].astype(F32) * scale
                product = gain[:, lanes] * grad_scaled[number, part, lanes] * normed
                mean = product if mean is None else mean + product
            if number == 0:
                mean_ref[part, :] = mean
            else:
                mean_ref[part, :] += mean
    mean = jnp.sum(mean_ref[...], axis=1, keepdims=True) / model
    mean_ref[...] = jnp.broadcast_to(mean, mean_ref.shape)

    stores = []
    for flip, step in blocks:
        number = flip * depth + step
        here = columns(plan, where, flip, step, cols)
        gain = gain_ref[:, here]
        for start in range(0, tokens, TILE):
            part = slice(start, start + TILE)
            scale = inverse[part, :]
            mean = mean_ref[part, :]
            for lane in range(0, cols, 128):
                lanes = slice(lane, lane + 128)
                normed = acts[flip, step, part, lanes].astype(F32) * scale
                gained = gain[:, lanes] * grad_scaled[number, part, lanes]
                out[number, part, lanes] = (scale * (gained - normed * mean)).astype(BF16)
        stores.append(fetch(out.at[number], out_ref.at[:, here], ends.at[number]))
    for store in stores:
        store.wait()


SMEM = pl.BlockSpec(memory_space=pltpu.SMEM)
VMEM = pl.BlockSpec(memory_space=pltpu.VMEM)
HBM = pl.BlockSpec(memory_space=pltpu.HBM)


def by_permutes(plan, activations, norm_gain, key_weight, key_grads):
    tokens, model = activations.shape
    key_width = key_grads.shape[1]
    rows, cols = key_width // plan.groups, model // plan.subs
    width, depth = plan.width, plan.depth
    gain = norm_gain.reshape(1, model)
    core, y, x, z = place(plan)
    where = jnp.stack([core, y, x, z]).astype(jnp.int32)
    shape = jax.ShapeDtypeStruct

    def to_core(core, y, x, z):
        return 1 - core, y, x, z

    def to_x(core, y, x, z):
        return core, y, x ^ 1, z

    def to_y(core, y, x, z):
        return core, y ^ 1, x, z

    def to_z(step):
        return lambda core, y, x, z: (core, y, x, z ^ step)

    def y_then(core, y, x, z):
        return (core, y ^ 1, x, z) if core == 0 else (core, y, x ^ 1, z)

    def x_then(core, y, x, z):
        return (core, y, x ^ 1, z) if core == 0 else (core, y ^ 1, x, z)

    def in_hbm(array):
        return pltpu.with_memory_space_constraint(array, pltpu.HBM)

    acts_hbm, grads_hbm, gain_hbm = in_hbm(activations), in_hbm(key_grads), in_hbm(gain)

    peer_acts = plan.send(activations, to_core)
    half_shape = (width * rows, tokens)
    scaled, mine, other, piece = pl.pallas_call(
        functools.partial(mine_kernel, plan),
        out_shape=(
            pltpu.VMEM((tokens, model), BF16),
            pltpu.VMEM(half_shape, BF16),
            pltpu.VMEM(half_shape, BF16),
            pltpu.VMEM((rows, cols), BF16),
        ),
        in_specs=[SMEM, HBM, HBM, HBM, HBM],
        out_specs=[VMEM] * 4,
        scratch_shapes=[
            pltpu.VMEM((tokens, model), BF16),
            pltpu.VMEM((tokens, key_width), BF16),
            pltpu.VMEM((1, model), F32),
            pltpu.VMEM((cols, key_width), BF16),
            pltpu.SemaphoreType.DMA((CHUNKS,)),
            pltpu.SemaphoreType.DMA((3,)),
        ],
        compiler_params=params(5),
        cost_estimate=cost(0, 8 * MIB),
        name="mine",
    )(where, acts_hbm, gain_hbm, grads_hbm, in_hbm(key_weight))
    theirs = plan.send(other, to_core)
    sent, kept, held = pl.pallas_call(
        functools.partial(term_kernel, plan),
        out_shape=(
            pltpu.VMEM((width * depth, rows, cols), BF16),
            pltpu.VMEM((depth, rows, cols), F32),
            pltpu.VMEM((depth, rows, cols), F32),
        ),
        in_specs=[SMEM, VMEM, HBM, VMEM, VMEM, VMEM],
        out_specs=[VMEM] * 3,
        scratch_shapes=[
            pltpu.VMEM((1, model), F32),
            pltpu.VMEM((tokens, model), BF16),
            pltpu.VMEM((2 * width * depth, rows, cols), F32),
            pltpu.SemaphoreType.DMA(()),
        ],
        compiler_params=params(8),
        cost_estimate=cost(4 * tokens * model * width * rows, 20 * MIB),
        name="term",
    )(where, peer_acts, gain_hbm, scaled, mine, theirs)
    got = plan.send(sent, y_then)

    acts, grads, inverse = pl.pallas_call(
        functools.partial(load_kernel, plan),
        out_shape=(
            pltpu.VMEM((2, depth, tokens, cols), BF16),
            pltpu.VMEM((tokens, key_width), BF16),
            pltpu.VMEM((tokens, 128), F32),
        ),
        in_specs=[SMEM, HBM, HBM],
        out_specs=[VMEM] * 3,
        scratch_shapes=[pltpu.SemaphoreType.DMA((3, depth))],
        compiler_params=params(1),
        cost_estimate=cost(0, 8 * MIB),
        name="load",
    )(where, acts_hbm, grads_hbm)

    planes = [plan.send(piece, to_z(step)) for step in range(1, depth)]
    got, planes[:-1], acts, grads, inverse = lax.optimization_barrier(
        (got, planes[:-1], acts, grads, inverse)
    )

    sent = pl.pallas_call(
        functools.partial(half_kernel, plan),
        out_shape=pltpu.VMEM((depth, rows, cols), BF16),
        in_specs=[SMEM, VMEM, VMEM],
        out_specs=VMEM,
        compiler_params=params(2),
        cost_estimate=cost(0, 2 * MIB),
        name="half",
    )(where, kept, got)
    again = plan.send(sent, x_then)

    own = pl.pallas_call(
        functools.partial(pack_kernel, plan),
        out_shape=pltpu.VMEM((depth, rows, cols), BF16),
        in_specs=[VMEM] * depth,
        out_specs=VMEM,
        compiler_params=params(1),
        cost_estimate=cost(0, MIB),
        name="pack",
    )(piece, *planes)
    own, _ = lax.optimization_barrier((own, sent))
    over = plan.send(own, x_then)
    mine_sent = jnp.concatenate([own, over])
    sums, gains, *sents = pl.pallas_call(
        functools.partial(plane_kernel, plan),
        out_shape=[pltpu.VMEM((rows, cols), F32), pltpu.VMEM((1, cols), F32)]
        + [pltpu.VMEM((rows + 16, cols), BF16)] * (depth - 1),
        in_specs=[SMEM] + [VMEM] * 5,
        out_specs=[VMEM] * (1 + depth),
        compiler_params=params(3),
        cost_estimate=cost(0, 2 * MIB),
        name="plane",
    )(where, held, got, own, again, gain)
    gots = [plan.send(array, to_z(step + 1)) for step, array in enumerate(sents)]
    mine_got = plan.send(mine_sent, y_then)
    weight_grads, gains = pl.pallas_call(
        functools.partial(last_kernel, plan),
        out_shape=(shape((rows, cols), F32), pltpu.VMEM((1, cols), F32)),
        in_specs=[VMEM] * (depth + 1),
        out_specs=(VMEM, VMEM),
        compiler_params=params(2),
        cost_estimate=cost(0, MIB),
        name="last",
    )(sums, gains, *gots)
    gains = gains + plan.send(gains, to_core)
    peer_first = plan.send(mine_sent[:EARLY], to_core)
    rest, gains = lax.optimization_barrier((mine_sent[EARLY:], gains))
    peer_rest = plan.send(rest, to_core)
    peer_gains = plan.send(gains, to_y)
    mine_got, peer_rest, peer_gains = lax.optimization_barrier((mine_got, peer_rest, peer_gains))
    peer_got = plan.send(mine_got, to_core)

    input_grads = pl.pallas_call(
        functools.partial(grad_kernel, plan),
        out_shape=shape((tokens, model), BF16),
        in_specs=[SMEM] + [VMEM] * 9,
        out_specs=HBM,
        scratch_shapes=[
            pltpu.VMEM((2 * depth, key_width, cols), BF16),
            pltpu.VMEM((2 * depth, tokens, cols), F32),
            pltpu.VMEM((tokens, 128), F32),
            pltpu.VMEM((2 * depth, tokens, cols), BF16),
            pltpu.SemaphoreType.DMA((2 * depth,)),
        ],
        compiler_params=params(12),
        cost_estimate=cost(2 * tokens * model * key_width, 8 * MIB),
        name="grad",
    )(where, acts, gain, grads, inverse, mine_sent, mine_got, peer_first, peer_rest, peer_got)
    return input_grads, weight_grads.T, (gains + peer_gains).reshape(cols) / plan.groups


def by_collectives(activations, norm_gain, key_weight, key_grads):
    inputs = activations.astype(F32)
    inverse_rms = lax.rsqrt(jnp.mean(inputs * inputs, axis=1, keepdims=True) + EPS)
    normed = inputs * inverse_rms
    scaled = (normed * norm_gain).astype(BF16)
    grad_scaled = lax.dot_general(
        key_grads,
        lax.all_gather(key_weight, "sub", axis=0, tiled=True),
        (((1,), (1,)), ((), ())),
        preferred_element_type=F32,
    )
    gained = norm_gain * grad_scaled
    input_grads = (
        inverse_rms * (gained - normed * jnp.mean(gained * normed, axis=1, keepdims=True))
    ).astype(BF16)
    groups = lax.axis_size("grp")
    cols = key_weight.shape[0]
    rows = key_grads.shape[1] // groups
    term = lax.dot_general(
        key_grads, scaled, (((0,), (0,)), ((), ())), preferred_element_type=F32
    )
    received = lax.all_to_all(term, "grp", split_axis=0, concat_axis=1, tiled=True)
    shared = jnp.sum(received.reshape(rows, groups, scaled.shape[1]), axis=1)
    owned = lax.psum_scatter(shared, "sub", scatter_dimension=1, tiled=True).T
    summed = lax.psum(jnp.sum(grad_scaled * normed, axis=0), AXES)
    gain_sum = lax.dynamic_slice_in_dim(summed, lax.axis_index("sub") * cols, cols)
    return input_grads, owned / groups, gain_sum / groups


def local(groups, subs, activations, norm_gain, key_weight, key_grads):
    cols = key_weight.shape[0]
    rows = key_grads.shape[1] // groups
    if groups == 4 and subs % 2 == 0 and subs & (subs - 1) == 0 and cols % 128 == 0 and rows % 16 == 0:
        plan = Plan(groups, subs)
        return by_permutes(plan, activations, norm_gain, key_weight, key_grads)
    return by_collectives(activations, norm_gain, key_weight, key_grads)


def solution(mesh):
    return jax.shard_map(
        functools.partial(local, mesh.shape["grp"], mesh.shape["sub"]),
        mesh=mesh,
        in_specs=(P(AXES, None), P(), P("sub", None), P(AXES, None)),
        out_specs=(P(AXES, None), P("sub", "grp"), P("sub")),
        check_vma=False,
    )
```

```python
import functools

import jax
import jax.numpy as jnp
from jax import lax
from jax.experimental import pallas as pl
from jax.experimental.pallas import tpu as pltpu
from jax.sharding import PartitionSpec as P

AXES = ("grp", "sub")
EPS = 1e-05
F32 = jnp.float32
BF16 = jnp.bfloat16
MIB = 1024 * 1024
TILE = 16
CHUNKS = 4
EARLY = 1


def params(limit):
    return pltpu.CompilerParams(vmem_limit_bytes=limit * MIB)


def cost(flops, moved):
    return pl.CostEstimate(flops=0, bytes_accessed=0, transcendentals=0)


class Plan:
    def __init__(self, groups, subs):
        self.groups, self.subs = groups, subs
        self.width = groups // 2
        self.depth = subs // self.width

    def index(self, core, y, x, z):
        return (y * 2 + core) * self.subs + z * self.width + x

    def pairs(self, move):
        found = []
        for core in range(2):
            for y in range(self.width):
                for x in range(self.width):
                    for z in range(self.depth):
                        found.append((self.index(core, y, x, z), self.index(*move(core, y, x, z))))
        return found

    def send(self, array, move):
        return lax.ppermute(array, AXES, self.pairs(move))


def place(plan):
    grp, sub = lax.axis_index("grp"), lax.axis_index("sub")
    return grp % 2, grp // 2, sub % plan.width, sub // plan.width


def slot_of(plan, where, first, second, to_z):
    core = where[0]
    to_x = jnp.where(core == 0, second, first)
    to_y = jnp.where(core == 0, first, second)
    return (to_x * plan.depth + to_z) * plan.width + to_y


def first_and_second(where):
    core, y, x = where[0], where[1], where[2]
    return jnp.where(core == 0, y, x), jnp.where(core == 0, x, y)


def fetch(source, target, sem):
    copy = pltpu.make_async_copy(source, target, sem)
    copy.start()
    return copy


def fetch_rows(source, target, sems):
    chunk = target.shape[0] // CHUNKS
    parts = [pl.ds(part * chunk, chunk) for part in range(CHUNKS)]
    return [fetch(source.at[part], target.at[part], sems.at[k]) for k, part in enumerate(parts)]


def scale_rows(source, gain, scaled, start, stop):
    @pl.loop(0, (stop - start) // TILE, unroll=8)
    def _(step):
        part = pl.ds(pl.multiple_of(start + step * TILE, TILE), TILE)
        inputs = source[part, :].astype(F32)
        inverse_rms = lax.rsqrt(jnp.mean(inputs * inputs, axis=1, keepdims=True) + EPS)
        scaled[part, :] = (inputs * inverse_rms * gain[...]).astype(BF16)


def mine_kernel(
    plan, where, acts_ref, gain_ref, grads_ref, weight_ref,
    scaled, mine, other, piece, acts, grads, gain, weight, sems, ends,
):
    core = where[0]
    tokens = acts.shape[0]
    rows = grads.shape[1] // plan.groups
    load = fetch(gain_ref, gain, ends.at[0])
    loads = fetch_rows(acts_ref, acts, sems)
    grads_load = fetch(grads_ref, grads, ends.at[1])
    weight_load = fetch(weight_ref, weight, ends.at[2])
    load.wait()
    chunk = tokens // CHUNKS
    for part in range(CHUNKS):
        loads[part].wait()
        scale_rows(acts, gain, scaled, part * chunk, (part + 1) * chunk)
    grads_load.wait()
    for half, (even, odd) in enumerate(((mine, other), (other, mine))):

        @pl.when(core == half)
        def _():
            for part in range(plan.width):
                place = slice(part * rows, (part + 1) * rows)
                column = 2 * part * rows
                even[place, :] = grads[:, column : column + rows].T
                odd[place, :] = grads[:, column + rows : column + 2 * rows].T

    weight_load.wait()
    for number in range(plan.groups):

        @pl.when(where[1] * 2 + core == number)
        def _():
            piece[...] = weight[:, number * rows : (number + 1) * rows].T


def peer_kernel(plan, acts, gain_ref, scaled, gain, end):
    fetch(gain_ref, gain, end).wait()
    scale_rows(acts, gain, scaled, 0, acts.shape[0])


def term_kernel(
    plan, where, scaled, peer_scaled, mine, theirs, sent_ref, kept_ref, held_ref, totals,
):
    width, depth = plan.width, plan.depth
    rows = mine.shape[0] // width
    cols = scaled.shape[1] // plan.subs

    for to_x in range(width):
        for to_z in range(depth):
            column = (to_z * width + to_x) * cols
            here = slice(column, column + cols)
            total = jnp.dot(mine[...], scaled[:, here], preferred_element_type=F32)
            total += jnp.dot(theirs[...], peer_scaled[:, here], preferred_element_type=F32)
            slot = (to_x * depth + to_z) * width
            for to_y in range(width):
                totals[slot + to_y] = total[to_y * rows : (to_y + 1) * rows]

    first, mine_second = first_and_second(where)
    for to_z in range(depth):
        for second in range(width):
            slot = slot_of(plan, where, 1 - first, second, to_z)
            sent_ref[second * depth + to_z] = totals[pl.ds(slot, 1)][0].astype(BF16)
        for second, out_ref in ((1 - mine_second, kept_ref), (mine_second, held_ref)):
            out_ref[to_z] = totals[pl.ds(slot_of(plan, where, first, second, to_z), 1)][0]


def half_kernel(plan, where, kept, got_ref, sent_ref):
    _, second = first_and_second(where)
    for to_z in range(plan.depth):
        block = kept[to_z] + got_ref[pl.ds((1 - second) * plan.depth + to_z, 1)][0].astype(F32)
        sent_ref[to_z] = block.astype(BF16)


def pack_kernel(plan, *refs):
    for number, ref in enumerate(refs[:-1]):
        refs[-1][number] = ref[...]


def plane_kernel(plan, where, held, got_ref, own, again_ref, gain_ref, sums_ref, gains_ref, *sent_refs):
    _, second = first_and_second(where)
    rows, cols = sums_ref.shape
    for step in range(plan.depth):
        plane = where[3] ^ step
        block = held[pl.ds(plane, 1)] + got_ref[pl.ds(second * plan.depth + plane, 1)].astype(F32)
        block = (block + again_ref[pl.ds(plane, 1)].astype(F32))[0]
        gains = jnp.sum(block * own[step].astype(F32), axis=0, keepdims=True)
        gains = gains / gain_ref[:, columns(plan, where, 0, step, cols)]
        if step == 0:
            sums_ref[...] = block
            gains_ref[...] = gains
        else:
            sent_refs[step - 1][:rows, :] = block.astype(BF16)
            row = lax.broadcasted_iota(jnp.int32, (16, cols), 0)
            tail = jnp.zeros((16, cols), F32)
            for number in range(3):
                high = gains.astype(BF16).astype(F32)
                tail = jnp.where(row == number, high, tail)
                gains = gains - high
            sent_refs[step - 1][rows:, :] = tail.astype(BF16)


def last_kernel(plan, sums_ref, gains_ref, *refs):
    got_refs, (out_ref, out_gains_ref) = refs[:-2], refs[-2:]
    rows = sums_ref.shape[0]
    total, gains = sums_ref[...], gains_ref[...]
    for ref in got_refs:
        total = total + ref[:rows, :].astype(F32)
        gains = gains + jnp.sum(ref[rows:, :].astype(F32), axis=0, keepdims=True)
    out_ref[...] = total / plan.groups
    out_gains_ref[...] = gains


def columns(plan, where, flip, step, cols):
    sub = (where[3] ^ step) * plan.width + (where[2] ^ flip)
    return pl.ds(pl.multiple_of(sub * cols, cols), cols)


def load_kernel(plan, where, acts_ref, grads_ref, acts, grads, inverse, sems):
    load = fetch(grads_ref, grads, sems.at[2, 0])
    cols = acts.shape[-1]
    copies = [
        fetch(acts_ref.at[:, columns(plan, where, flip, step, cols)], acts.at[flip, step], sems.at[flip, step])
        for flip in range(2)
        for step in range(plan.depth)
    ]
    load.wait()
    tokens = grads.shape[0]
    for number, copy in enumerate(copies):
        copy.wait()
        block = acts.at[number // plan.depth, number % plan.depth]
        for start in range(0, tokens, TILE):
            part = slice(start, start + TILE)
            square = None
            for lane in range(0, cols, 128):
                inputs = block[part, lane : lane + 128].astype(F32)
                square = inputs * inputs if square is None else square + inputs * inputs
            if number == 0:
                inverse[part, :] = square
            else:
                inverse[part, :] += square
    mean_square = jnp.sum(inverse[...], axis=1, keepdims=True) / (2 * plan.depth * cols)
    inverse[...] = jnp.broadcast_to(lax.rsqrt(mean_square + EPS), inverse.shape)


def place_weight(plan, where, pieces, from_core, second, weight):
    depth = plan.depth
    blocks = [array.at[number] for array in pieces for number in range(array.shape[0])]
    rows = blocks[0].shape[0]
    for part in range(2):
        if second:
            flip = from_core if part == 0 else 1
            far_y = (1 - from_core) if part == 0 else 1
        else:
            flip = 0 if part == 0 else 1 - from_core
            far_y = 0 if part == 0 else from_core
        grp = (where[1] ^ far_y) * 2 + from_core
        here = pl.ds(pl.multiple_of(grp * rows, rows), rows)
        for step in range(depth):
            weight[pl.ds(flip * depth + step, 1), here] = blocks[part * depth + step][...][None]


def grad_kernel(
    plan, where, acts, gain_ref, grads, inverse,
    own, over, own_got, over_got, peer_own, peer_first, peer_over, peer_own_first, peer_own_rest, peer_over_got,
    out_ref, weight, grad_scaled, mean_ref, out, ends,
):
    core = where[0]
    depth = plan.depth
    tokens, cols = acts.shape[2:]
    model = cols * plan.subs
    place_weight(plan, where, [own, over], core, False, weight)
    place_weight(plan, where, [peer_own, peer_first, peer_over], 1 - core, False, weight)
    place_weight(plan, where, [own_got, over_got], core, True, weight)
    place_weight(plan, where, [peer_own_first, peer_own_rest, peer_over_got], 1 - core, True, weight)
    blocks = [(flip, step) for flip in range(2) for step in range(depth)]

    def multiply(number):
        grad_scaled[number] = jnp.dot(grads[...], weight[number], preferred_element_type=F32)

    def add_mean(number):
        flip, step = blocks[number]
        gain = gain_ref[:, columns(plan, where, flip, step, cols)]
        for start in range(0, tokens, TILE):
            part = slice(start, start + TILE)
            mean = None
            for lane in range(0, cols, 128):
                lanes = slice(lane, lane + 128)
                product = gain[:, lanes] * grad_scaled[number, part, lanes]
                product = product * acts[flip, step, part, lanes].astype(F32)
                mean = product if mean is None else mean + product
            if number == 0:
                mean_ref[part, :] = mean
            else:
                mean_ref[part, :] += mean

    multiply(0)
    for number in range(1, len(blocks)):
        multiply(number)
        add_mean(number - 1)
    add_mean(len(blocks) - 1)
    mean = jnp.sum(mean_ref[...], axis=1, keepdims=True) / model
    scale = inverse[...]
    mean_ref[...] = mean * scale * scale * scale

    stores = []
    big = tokens // CHUNKS
    for base in range(0, tokens, big):
        for flip, step in blocks:
            number = flip * depth + step
            here = columns(plan, where, flip, step, cols)
            gain = gain_ref[:, here]
            for start in range(base, base + big, TILE):
                part = slice(start, start + TILE)
                scale = inverse[part, :]
                mean = mean_ref[part, :]
                tiles = []
                for lane in range(0, cols, 128):
                    lanes = slice(lane, lane + 128)
                    inputs = acts[flip, step, part, lanes].astype(F32)
                    gained = gain[:, lanes] * grad_scaled[number, part, lanes]
                    tiles.append((scale * gained - inputs * mean).astype(BF16))
                out[part, here] = jnp.concatenate(tiles, axis=1)
        rows_here = pl.ds(base, big)
        stores.append(fetch(out.at[rows_here], out_ref.at[rows_here], ends.at[base // big]))
    for store in stores:
        store.wait()


SMEM = pl.BlockSpec(memory_space=pltpu.SMEM)
VMEM = pl.BlockSpec(memory_space=pltpu.VMEM)
HBM = pl.BlockSpec(memory_space=pltpu.HBM)


def by_permutes(plan, activations, norm_gain, key_weight, key_grads):
    tokens, model = activations.shape
    key_width = key_grads.shape[1]
    rows, cols = key_width // plan.groups, model // plan.subs
    width, depth = plan.width, plan.depth
    gain = norm_gain.reshape(1, model)
    core, y, x, z = place(plan)
    where = jnp.stack([core, y, x, z]).astype(jnp.int32)
    shape = jax.ShapeDtypeStruct

    def to_core(core, y, x, z):
        return 1 - core, y, x, z

    def to_x(core, y, x, z):
        return core, y, x ^ 1, z

    def to_y(core, y, x, z):
        return core, y ^ 1, x, z

    def to_z(step):
        return lambda core, y, x, z: (core, y, x, z ^ step)

    def y_then(core, y, x, z):
        return (core, y ^ 1, x, z) if core == 0 else (core, y, x ^ 1, z)

    def x_then(core, y, x, z):
        return (core, y, x ^ 1, z) if core == 0 else (core, y ^ 1, x, z)

    def in_hbm(array):
        return pltpu.with_memory_space_constraint(array, pltpu.HBM)

    acts_hbm, grads_hbm, gain_hbm = in_hbm(activations), in_hbm(key_grads), in_hbm(gain)

    peer_acts = plan.send(activations, to_core)
    half_shape = (width * rows, tokens)
    scaled, mine, other, piece = pl.pallas_call(
        functools.partial(mine_kernel, plan),
        out_shape=(
            pltpu.VMEM((tokens, model), BF16),
            pltpu.VMEM(half_shape, BF16),
            pltpu.VMEM(half_shape, BF16),
            pltpu.VMEM((rows, cols), BF16),
        ),
        in_specs=[SMEM, HBM, HBM, HBM, HBM],
        out_specs=[VMEM] * 4,
        scratch_shapes=[
            pltpu.VMEM((tokens, model), BF16),
            pltpu.VMEM((tokens, key_width), BF16),
            pltpu.VMEM((1, model), F32),
            pltpu.VMEM((cols, key_width), BF16),
            pltpu.SemaphoreType.DMA((CHUNKS,)),
            pltpu.SemaphoreType.DMA((3,)),
        ],
        compiler_params=params(5),
        cost_estimate=cost(0, 8 * MIB),
        name="mine",
    )(where, acts_hbm, gain_hbm, grads_hbm, in_hbm(key_weight))
    theirs = plan.send(other, to_core)
    peer_scaled = pl.pallas_call(
        functools.partial(peer_kernel, plan),
        out_shape=pltpu.VMEM((tokens, model), BF16),
        in_specs=[VMEM, HBM],
        out_specs=VMEM,
        scratch_shapes=[pltpu.VMEM((1, model), F32), pltpu.SemaphoreType.DMA(())],
        compiler_params=params(2),
        cost_estimate=cost(0, 2 * MIB),
        name="peer",
    )(peer_acts, gain_hbm)
    theirs, _ = lax.optimization_barrier((theirs, peer_scaled))
    sent, kept, held = pl.pallas_call(
        functools.partial(term_kernel, plan),
        out_shape=(
            pltpu.VMEM((width * depth, rows, cols), BF16),
            pltpu.VMEM((depth, rows, cols), F32),
            pltpu.VMEM((depth, rows, cols), F32),
        ),
        in_specs=[SMEM] + [VMEM] * 4,
        out_specs=[VMEM] * 3,
        scratch_shapes=[pltpu.VMEM((2 * width * depth, rows, cols), F32)],
        compiler_params=params(6),
        cost_estimate=cost(4 * tokens * model * width * rows, 20 * MIB),
        name="term",
    )(where, scaled, peer_scaled, mine, theirs)
    got = plan.send(sent, y_then)

    acts, grads, inverse = pl.pallas_call(
        functools.partial(load_kernel, plan),
        out_shape=(
            pltpu.VMEM((2, depth, tokens, cols), BF16),
            pltpu.VMEM((tokens, key_width), BF16),
            pltpu.VMEM((tokens, 128), F32),
        ),
        in_specs=[SMEM, HBM, HBM],
        out_specs=[VMEM] * 3,
        scratch_shapes=[pltpu.SemaphoreType.DMA((3, depth))],
        compiler_params=params(1),
        cost_estimate=cost(0, 8 * MIB),
        name="load",
    )(where, acts_hbm, grads_hbm)

    planes = [plan.send(piece, to_z(step)) for step in range(1, depth)]
    got, planes[1], acts, grads, inverse = lax.optimization_barrier(
        (got, planes[1], acts, grads, inverse)
    )

    sent = pl.pallas_call(
        functools.partial(half_kernel, plan),
        out_shape=pltpu.VMEM((depth, rows, cols), BF16),
        in_specs=[SMEM, VMEM, VMEM],
        out_specs=VMEM,
        compiler_params=params(2),
        cost_estimate=cost(0, 2 * MIB),
        name="half",
    )(where, kept, got)
    sent, planes = lax.optimization_barrier((sent, planes))
    again = plan.send(sent, x_then)

    own = pl.pallas_call(
        functools.partial(pack_kernel, plan),
        out_shape=pltpu.VMEM((depth, rows, cols), BF16),
        in_specs=[VMEM] * depth,
        out_specs=VMEM,
        compiler_params=params(1),
        cost_estimate=cost(0, MIB),
        name="pack",
    )(piece, *planes)
    own, _ = lax.optimization_barrier((own, sent))
    over = plan.send(own, x_then)
    sums, gains, *sents = pl.pallas_call(
        functools.partial(plane_kernel, plan),
        out_shape=[pltpu.VMEM((rows, cols), F32), pltpu.VMEM((1, cols), F32)]
        + [pltpu.VMEM((rows + 16, cols), BF16)] * (depth - 1),
        in_specs=[SMEM] + [VMEM] * 5,
        out_specs=[VMEM] * (1 + depth),
        compiler_params=params(3),
        cost_estimate=cost(0, 2 * MIB),
        name="plane",
    )(where, held, got, own, again, gain)
    gots = [plan.send(array, to_z(step + 1)) for step, array in enumerate(sents)]
    first, _ = lax.optimization_barrier((own, again))
    own_got = plan.send(first, y_then)
    over_got = plan.send(over, y_then)
    weight_grads, gains = pl.pallas_call(
        functools.partial(last_kernel, plan),
        out_shape=(shape((rows, cols), F32), pltpu.VMEM((1, cols), F32)),
        in_specs=[VMEM] * (depth + 1),
        out_specs=(VMEM, VMEM),
        compiler_params=params(2),
        cost_estimate=cost(0, MIB),
        name="last",
    )(sums, gains, *gots)
    peer_own = plan.send(own, to_core)
    peer_first = plan.send(over[: 2 * EARLY], to_core)
    rest, gains = lax.optimization_barrier((over[2 * EARLY :], gains))
    peer_over = plan.send(rest, to_core)
    gains = gains + plan.send(gains, to_core)
    peer_own_first = plan.send(own_got[: depth - 1], to_core)
    over_got, peer_over, peer_own_first, gains = lax.optimization_barrier(
        (over_got, peer_over, peer_own_first, gains)
    )
    peer_over_got = plan.send(over_got, to_core)
    peer_own_rest = plan.send(own_got[depth - 1 :], to_core)
    peer_gains = plan.send(gains, to_y)

    input_grads = pl.pallas_call(
        functools.partial(grad_kernel, plan),
        out_shape=shape((tokens, model), BF16),
        in_specs=[SMEM] + [VMEM] * 14,
        out_specs=HBM,
        scratch_shapes=[
            pltpu.VMEM((2 * depth, key_width, cols), BF16),
            pltpu.VMEM((2 * depth, tokens, cols), F32),
            pltpu.VMEM((tokens, 128), F32),
            pltpu.VMEM((tokens, model), BF16),
            pltpu.SemaphoreType.DMA((CHUNKS,)),
        ],
        compiler_params=params(12),
        cost_estimate=cost(2 * tokens * model * key_width, 8 * MIB),
        name="grad",
    )(
        where, acts, gain, grads, inverse,
        own, over, own_got, over_got, peer_own, peer_first, peer_over, peer_own_first, peer_own_rest, peer_over_got,
    )
    peer_gains, input_grads = lax.optimization_barrier((peer_gains, input_grads))
    return input_grads, weight_grads.T, (gains + peer_gains).reshape(cols) / plan.groups


def by_collectives(activations, norm_gain, key_weight, key_grads):
    inputs = activations.astype(F32)
    inverse_rms = lax.rsqrt(jnp.mean(inputs * inputs, axis=1, keepdims=True) + EPS)
    normed = inputs * inverse_rms
    scaled = (normed * norm_gain).astype(BF16)
    grad_scaled = lax.dot_general(
        key_grads,
        lax.all_gather(key_weight, "sub", axis=0, tiled=True),
        (((1,), (1,)), ((), ())),
        preferred_element_type=F32,
    )
    gained = norm_gain * grad_scaled
    input_grads = (
        inverse_rms * (gained - normed * jnp.mean(gained * normed, axis=1, keepdims=True))
    ).astype(BF16)
    groups = lax.axis_size("grp")
    cols = key_weight.shape[0]
    rows = key_grads.shape[1] // groups
    term = lax.dot_general(
        key_grads, scaled, (((0,), (0,)), ((), ())), preferred_element_type=F32
    )
    received = lax.all_to_all(term, "grp", split_axis=0, concat_axis=1, tiled=True)
    shared = jnp.sum(received.reshape(rows, groups, scaled.shape[1]), axis=1)
    owned = lax.psum_scatter(shared, "sub", scatter_dimension=1, tiled=True).T
    summed = lax.psum(jnp.sum(grad_scaled * normed, axis=0), AXES)
    gain_sum = lax.dynamic_slice_in_dim(summed, lax.axis_index("sub") * cols, cols)
    return input_grads, owned / groups, gain_sum / groups


def local(groups, subs, activations, norm_gain, key_weight, key_grads):
    cols = key_weight.shape[0]
    rows = key_grads.shape[1] // groups
    if groups == 4 and subs % 2 == 0 and subs & (subs - 1) == 0 and cols % 128 == 0 and rows % 16 == 0:
        plan = Plan(groups, subs)
        return by_permutes(plan, activations, norm_gain, key_weight, key_grads)
    return by_collectives(activations, norm_gain, key_weight, key_grads)


def solution(mesh):
    return jax.shard_map(
        functools.partial(local, mesh.shape["grp"], mesh.shape["sub"]),
        mesh=mesh,
        in_specs=(P(AXES, None), P(), P("sub", None), P(AXES, None)),
        out_specs=(P(AXES, None), P("sub", "grp"), P("sub")),
        check_vma=False,
    )
```

```python
import functools

import jax
import jax.numpy as jnp
from jax import lax
from jax.experimental import pallas as pl
from jax.experimental.pallas import tpu as pltpu
from jax.sharding import PartitionSpec as P

AXES = ("grp", "sub")
EPS = 1e-05
F32 = jnp.float32
BF16 = jnp.bfloat16
MIB = 1024 * 1024
TILE = 16
CHUNKS = 4
EARLY = 1


def params(limit):
    return pltpu.CompilerParams(vmem_limit_bytes=limit * MIB)


def cost(flops, moved):
    return pl.CostEstimate(flops=0, bytes_accessed=0, transcendentals=0)


class Plan:
    def __init__(self, groups, subs):
        self.groups, self.subs = groups, subs
        self.width = groups // 2
        self.depth = subs // self.width

    def index(self, core, y, x, z):
        return (y * 2 + core) * self.subs + z * self.width + x

    def pairs(self, move):
        found = []
        for core in range(2):
            for y in range(self.width):
                for x in range(self.width):
                    for z in range(self.depth):
                        found.append((self.index(core, y, x, z), self.index(*move(core, y, x, z))))
        return found

    def send(self, array, move):
        return lax.ppermute(array, AXES, self.pairs(move))


def place(plan):
    grp, sub = lax.axis_index("grp"), lax.axis_index("sub")
    return grp % 2, grp // 2, sub % plan.width, sub // plan.width


def slot_of(plan, where, first, second, to_z):
    core = where[0]
    to_x = jnp.where(core == 0, second, first)
    to_y = jnp.where(core == 0, first, second)
    return (to_x * plan.depth + to_z) * plan.width + to_y


def first_and_second(where):
    core, y, x = where[0], where[1], where[2]
    return jnp.where(core == 0, y, x), jnp.where(core == 0, x, y)


def fetch(source, target, sem):
    copy = pltpu.make_async_copy(source, target, sem)
    copy.start()
    return copy


def fetch_rows(source, target, sems):
    chunk = target.shape[0] // CHUNKS
    parts = [pl.ds(part * chunk, chunk) for part in range(CHUNKS)]
    return [fetch(source.at[part], target.at[part], sems.at[k]) for k, part in enumerate(parts)]


def scale_rows(source, gain, scaled, start, stop):
    @pl.loop(0, (stop - start) // TILE, unroll=8)
    def _(step):
        part = pl.ds(pl.multiple_of(start + step * TILE, TILE), TILE)
        inputs = source[part, :].astype(F32)
        inverse_rms = lax.rsqrt(jnp.mean(inputs * inputs, axis=1, keepdims=True) + EPS)
        scaled[part, :] = (inputs * inverse_rms * gain[...]).astype(BF16)


def mine_kernel(
    plan, where, acts_ref, gain_ref, grads_ref, weight_ref,
    scaled, mine, other, piece, gain, acts, grads, weight, sems, ends,
):
    core = where[0]
    tokens = acts.shape[0]
    rows = grads.shape[1] // plan.groups
    load = fetch(gain_ref, gain, ends.at[0])
    loads = fetch_rows(acts_ref, acts, sems)
    grads_load = fetch(grads_ref, grads, ends.at[1])
    weight_load = fetch(weight_ref, weight, ends.at[2])
    load.wait()
    chunk = tokens // CHUNKS
    for part in range(CHUNKS):
        loads[part].wait()
        scale_rows(acts, gain, scaled, part * chunk, (part + 1) * chunk)
    grads_load.wait()
    for half, (even, odd) in enumerate(((mine, other), (other, mine))):

        @pl.when(core == half)
        def _():
            for part in range(plan.width):
                place = slice(part * rows, (part + 1) * rows)
                column = 2 * part * rows
                even[place, :] = grads[:, column : column + rows].T
                odd[place, :] = grads[:, column + rows : column + 2 * rows].T

    weight_load.wait()
    for number in range(plan.groups):

        @pl.when(where[1] * 2 + core == number)
        def _():
            piece[...] = weight[:, number * rows : (number + 1) * rows].T


def peer_kernel(plan, acts, gain, scaled):
    scale_rows(acts, gain, scaled, 0, acts.shape[0])


def term_kernel(
    plan, where, scaled, peer_scaled, mine, theirs, sent_ref, kept_ref, held_ref, totals,
):
    width, depth = plan.width, plan.depth
    rows = mine.shape[0] // width
    cols = scaled.shape[1] // plan.subs

    for to_x in range(width):
        for to_z in range(depth):
            column = (to_z * width + to_x) * cols
            here = slice(column, column + cols)
            total = jnp.dot(mine[...], scaled[:, here], preferred_element_type=F32)
            total += jnp.dot(theirs[...], peer_scaled[:, here], preferred_element_type=F32)
            slot = (to_x * depth + to_z) * width
            for to_y in range(width):
                totals[slot + to_y] = total[to_y * rows : (to_y + 1) * rows]

    first, mine_second = first_and_second(where)
    for to_z in range(depth):
        for second in range(width):
            slot = slot_of(plan, where, 1 - first, second, to_z)
            sent_ref[second * depth + to_z] = totals[pl.ds(slot, 1)][0].astype(BF16)
        for second, out_ref in ((1 - mine_second, kept_ref), (mine_second, held_ref)):
            out_ref[to_z] = totals[pl.ds(slot_of(plan, where, first, second, to_z), 1)][0]


def half_kernel(plan, where, kept, got_ref, sent_ref):
    _, second = first_and_second(where)
    for to_z in range(plan.depth):
        block = kept[to_z] + got_ref[pl.ds((1 - second) * plan.depth + to_z, 1)][0].astype(F32)
        sent_ref[to_z] = block.astype(BF16)


def pack_kernel(plan, *refs):
    for number, ref in enumerate(refs[:-1]):
        refs[-1][number] = ref[...]


def plane_kernel(plan, where, held, got_ref, own, again_ref, gain_ref, sums_ref, gains_ref, *sent_refs):
    _, second = first_and_second(where)
    rows, cols = sums_ref.shape
    for step in range(plan.depth):
        plane = where[3] ^ step
        block = held[pl.ds(plane, 1)] + got_ref[pl.ds(second * plan.depth + plane, 1)].astype(F32)
        block = (block + again_ref[pl.ds(plane, 1)].astype(F32))[0]
        gains = jnp.sum(block * own[step].astype(F32), axis=0, keepdims=True)
        gains = gains / gain_ref[:, columns(plan, where, 0, step, cols)]
        if step == 0:
            sums_ref[...] = block
            gains_ref[...] = gains
        else:
            sent_refs[step - 1][:rows, :] = block.astype(BF16)
            row = lax.broadcasted_iota(jnp.int32, (16, cols), 0)
            tail = jnp.zeros((16, cols), F32)
            for number in range(3):
                high = gains.astype(BF16).astype(F32)
                tail = jnp.where(row == number, high, tail)
                gains = gains - high
            sent_refs[step - 1][rows:, :] = tail.astype(BF16)


def last_kernel(plan, sums_ref, gains_ref, *refs):
    got_refs, (out_ref, out_gains_ref) = refs[:-2], refs[-2:]
    rows = sums_ref.shape[0]
    total, gains = sums_ref[...], gains_ref[...]
    for ref in got_refs:
        total = total + ref[:rows, :].astype(F32)
        gains = gains + jnp.sum(ref[rows:, :].astype(F32), axis=0, keepdims=True)
    out_ref[...] = total / plan.groups
    out_gains_ref[...] = gains


def columns(plan, where, flip, step, cols):
    sub = (where[3] ^ step) * plan.width + (where[2] ^ flip)
    return pl.ds(pl.multiple_of(sub * cols, cols), cols)


def load_kernel(plan, where, acts_ref, grads_ref, acts, grads, inverse, sems):
    load = fetch(grads_ref, grads, sems.at[2, 0])
    cols = acts.shape[-1]
    copies = [
        fetch(acts_ref.at[:, columns(plan, where, flip, step, cols)], acts.at[flip, step], sems.at[flip, step])
        for flip in range(2)
        for step in range(plan.depth)
    ]
    load.wait()
    tokens = grads.shape[0]
    for number, copy in enumerate(copies):
        copy.wait()
        block = acts.at[number // plan.depth, number % plan.depth]
        for start in range(0, tokens, TILE):
            part = slice(start, start + TILE)
            square = None
            for lane in range(0, cols, 128):
                inputs = block[part, lane : lane + 128].astype(F32)
                square = inputs * inputs if square is None else square + inputs * inputs
            if number == 0:
                inverse[part, :] = square
            else:
                inverse[part, :] += square
    mean_square = jnp.sum(inverse[...], axis=1, keepdims=True) / (2 * plan.depth * cols)
    inverse[...] = jnp.broadcast_to(lax.rsqrt(mean_square + EPS), inverse.shape)


def place_weight(plan, where, pieces, from_core, second, weight):
    depth = plan.depth
    blocks = [array.at[number] for array in pieces for number in range(array.shape[0])]
    rows = blocks[0].shape[0]
    for part in range(2):
        if second:
            flip = from_core if part == 0 else 1
            far_y = (1 - from_core) if part == 0 else 1
        else:
            flip = 0 if part == 0 else 1 - from_core
            far_y = 0 if part == 0 else from_core
        grp = (where[1] ^ far_y) * 2 + from_core
        here = pl.ds(pl.multiple_of(grp * rows, rows), rows)
        for step in range(depth):
            weight[pl.ds(flip * depth + step, 1), here] = blocks[part * depth + step][...][None]


def grad_kernel(
    plan, where, acts, gain_ref, grads, inverse,
    own, over, own_got, over_got, peer_own, peer_first, peer_over, peer_own_first, peer_own_rest, peer_over_got,
    out_ref, weight, grad_scaled, mean_ref, out, ends,
):
    core = where[0]
    depth = plan.depth
    tokens, cols = acts.shape[2:]
    model = cols * plan.subs
    place_weight(plan, where, [own, over], core, False, weight)
    place_weight(plan, where, [peer_own, peer_first, peer_over], 1 - core, False, weight)
    place_weight(plan, where, [own_got, over_got], core, True, weight)
    place_weight(plan, where, [peer_own_first, peer_own_rest, peer_over_got], 1 - core, True, weight)
    blocks = [(flip, step) for flip in range(2) for step in range(depth)]

    def multiply(number):
        grad_scaled[number] = jnp.dot(grads[...], weight[number], preferred_element_type=F32)

    def add_mean(number):
        flip, step = blocks[number]
        gain = gain_ref[:, columns(plan, where, flip, step, cols)]
        for start in range(0, tokens, TILE):
            part = slice(start, start + TILE)
            mean = None
            for lane in range(0, cols, 128):
                lanes = slice(lane, lane + 128)
                product = gain[:, lanes] * grad_scaled[number, part, lanes]
                product = product * acts[flip, step, part, lanes].astype(F32)
                mean = product if mean is None else mean + product
            if number == 0:
                mean_ref[part, :] = mean
            else:
                mean_ref[part, :] += mean

    multiply(0)
    for number in range(1, len(blocks)):
        multiply(number)
        add_mean(number - 1)
    add_mean(len(blocks) - 1)
    mean = jnp.sum(mean_ref[...], axis=1, keepdims=True) / model
    scale = inverse[...]
    mean_ref[...] = mean * scale * scale * scale

    stores = []
    big = tokens // CHUNKS
    for base in range(0, tokens, big):
        for flip, step in blocks:
            number = flip * depth + step
            here = columns(plan, where, flip, step, cols)
            gain = gain_ref[:, here]
            for start in range(base, base + big, TILE):
                part = slice(start, start + TILE)
                scale = inverse[part, :]
                mean = mean_ref[part, :]
                tiles = []
                for lane in range(0, cols, 128):
                    lanes = slice(lane, lane + 128)
                    inputs = acts[flip, step, part, lanes].astype(F32)
                    gained = gain[:, lanes] * grad_scaled[number, part, lanes]
                    tiles.append((scale * gained - inputs * mean).astype(BF16))
                out[part, here] = jnp.concatenate(tiles, axis=1)
        rows_here = pl.ds(base, big)
        stores.append(fetch(out.at[rows_here], out_ref.at[rows_here], ends.at[base // big]))
    for store in stores:
        store.wait()


SMEM = pl.BlockSpec(memory_space=pltpu.SMEM)
VMEM = pl.BlockSpec(memory_space=pltpu.VMEM)
HBM = pl.BlockSpec(memory_space=pltpu.HBM)


def by_permutes(plan, activations, norm_gain, key_weight, key_grads):
    tokens, model = activations.shape
    key_width = key_grads.shape[1]
    rows, cols = key_width // plan.groups, model // plan.subs
    width, depth = plan.width, plan.depth
    gain = norm_gain.reshape(1, model)
    core, y, x, z = place(plan)
    where = jnp.stack([core, y, x, z]).astype(jnp.int32)
    shape = jax.ShapeDtypeStruct

    def to_core(core, y, x, z):
        return 1 - core, y, x, z

    def to_x(core, y, x, z):
        return core, y, x ^ 1, z

    def to_y(core, y, x, z):
        return core, y ^ 1, x, z

    def to_z(step):
        return lambda core, y, x, z: (core, y, x, z ^ step)

    def y_then(core, y, x, z):
        return (core, y ^ 1, x, z) if core == 0 else (core, y, x ^ 1, z)

    def x_then(core, y, x, z):
        return (core, y, x ^ 1, z) if core == 0 else (core, y ^ 1, x, z)

    def in_hbm(array):
        return pltpu.with_memory_space_constraint(array, pltpu.HBM)

    acts_hbm, grads_hbm, gain_hbm = in_hbm(activations), in_hbm(key_grads), in_hbm(gain)

    peer_acts = plan.send(activations, to_core)
    half_shape = (width * rows, tokens)
    scaled, mine, other, piece, near_gain = pl.pallas_call(
        functools.partial(mine_kernel, plan),
        out_shape=(
            pltpu.VMEM((tokens, model), BF16),
            pltpu.VMEM(half_shape, BF16),
            pltpu.VMEM(half_shape, BF16),
            pltpu.VMEM((rows, cols), BF16),
            pltpu.VMEM((1, model), F32),
        ),
        in_specs=[SMEM, HBM, HBM, HBM, HBM],
        out_specs=[VMEM] * 5,
        scratch_shapes=[
            pltpu.VMEM((tokens, model), BF16),
            pltpu.VMEM((tokens, key_width), BF16),
            pltpu.VMEM((cols, key_width), BF16),
            pltpu.SemaphoreType.DMA((CHUNKS,)),
            pltpu.SemaphoreType.DMA((3,)),
        ],
        compiler_params=params(5),
        cost_estimate=cost(0, 8 * MIB),
        name="mine",
    )(where, acts_hbm, gain_hbm, grads_hbm, in_hbm(key_weight))
    theirs = plan.send(other, to_core)
    peer_scaled = pl.pallas_call(
        functools.partial(peer_kernel, plan),
        out_shape=pltpu.VMEM((tokens, model), BF16),
        in_specs=[VMEM, VMEM],
        out_specs=VMEM,
        compiler_params=params(2),
        cost_estimate=cost(0, 2 * MIB),
        name="peer",
    )(peer_acts, near_gain)
    theirs, _ = lax.optimization_barrier((theirs, peer_scaled))
    sent, kept, held = pl.pallas_call(
        functools.partial(term_kernel, plan),
        out_shape=(
            pltpu.VMEM((width * depth, rows, cols), BF16),
            pltpu.VMEM((depth, rows, cols), F32),
            pltpu.VMEM((depth, rows, cols), F32),
        ),
        in_specs=[SMEM] + [VMEM] * 4,
        out_specs=[VMEM] * 3,
        scratch_shapes=[pltpu.VMEM((2 * width * depth, rows, cols), F32)],
        compiler_params=params(6),
        cost_estimate=cost(4 * tokens * model * width * rows, 20 * MIB),
        name="term",
    )(where, scaled, peer_scaled, mine, theirs)
    got = plan.send(sent, y_then)

    acts, grads, inverse = pl.pallas_call(
        functools.partial(load_kernel, plan),
        out_shape=(
            pltpu.VMEM((2, depth, tokens, cols), BF16),
            pltpu.VMEM((tokens, key_width), BF16),
            pltpu.VMEM((tokens, 128), F32),
        ),
        in_specs=[SMEM, HBM, HBM],
        out_specs=[VMEM] * 3,
        scratch_shapes=[pltpu.SemaphoreType.DMA((3, depth))],
        compiler_params=params(1),
        cost_estimate=cost(0, 8 * MIB),
        name="load",
    )(where, acts_hbm, grads_hbm)

    planes = [plan.send(piece, to_z(step)) for step in range(1, depth)]
    got, planes[1], acts, grads, inverse = lax.optimization_barrier(
        (got, planes[1], acts, grads, inverse)
    )

    sent = pl.pallas_call(
        functools.partial(half_kernel, plan),
        out_shape=pltpu.VMEM((depth, rows, cols), BF16),
        in_specs=[SMEM, VMEM, VMEM],
        out_specs=VMEM,
        compiler_params=params(2),
        cost_estimate=cost(0, 2 * MIB),
        name="half",
    )(where, kept, got)
    sent, planes = lax.optimization_barrier((sent, planes))
    again = plan.send(sent, x_then)

    own = pl.pallas_call(
        functools.partial(pack_kernel, plan),
        out_shape=pltpu.VMEM((depth, rows, cols), BF16),
        in_specs=[VMEM] * depth,
        out_specs=VMEM,
        compiler_params=params(1),
        cost_estimate=cost(0, MIB),
        name="pack",
    )(piece, *planes)
    own, _ = lax.optimization_barrier((own, sent))
    over = plan.send(own, x_then)
    sums, gains, *sents = pl.pallas_call(
        functools.partial(plane_kernel, plan),
        out_shape=[pltpu.VMEM((rows, cols), F32), pltpu.VMEM((1, cols), F32)]
        + [pltpu.VMEM((rows + 16, cols), BF16)] * (depth - 1),
        in_specs=[SMEM] + [VMEM] * 5,
        out_specs=[VMEM] * (1 + depth),
        compiler_params=params(3),
        cost_estimate=cost(0, 2 * MIB),
        name="plane",
    )(where, held, got, own, again, gain)
    gots = [plan.send(array, to_z(step + 1)) for step, array in enumerate(sents)]
    first, _ = lax.optimization_barrier((own, again))
    own_got = plan.send(first, y_then)
    over_got = plan.send(over, y_then)
    weight_grads, gains = pl.pallas_call(
        functools.partial(last_kernel, plan),
        out_shape=(shape((rows, cols), F32), pltpu.VMEM((1, cols), F32)),
        in_specs=[VMEM] * (depth + 1),
        out_specs=(VMEM, VMEM),
        compiler_params=params(2),
        cost_estimate=cost(0, MIB),
        name="last",
    )(sums, gains, *gots)
    peer_own = plan.send(own, to_core)
    peer_first = plan.send(over[: 2 * EARLY], to_core)
    rest, gains = lax.optimization_barrier((over[2 * EARLY :], gains))
    peer_over = plan.send(rest, to_core)
    gains = gains + plan.send(gains, to_core)
    peer_own_first = plan.send(own_got[: depth - 1], to_core)
    over_got, peer_over, peer_own_first, gains = lax.optimization_barrier(
        (over_got, peer_over, peer_own_first, gains)
    )
    peer_over_got = plan.send(over_got, to_core)
    peer_own_rest = plan.send(own_got[depth - 1 :], to_core)
    peer_gains = plan.send(gains, to_y)

    input_grads = pl.pallas_call(
        functools.partial(grad_kernel, plan),
        out_shape=shape((tokens, model), BF16),
        in_specs=[SMEM] + [VMEM] * 14,
        out_specs=HBM,
        scratch_shapes=[
            pltpu.VMEM((2 * depth, key_width, cols), BF16),
            pltpu.VMEM((2 * depth, tokens, cols), F32),
            pltpu.VMEM((tokens, 128), F32),
            pltpu.VMEM((tokens, model), BF16),
            pltpu.SemaphoreType.DMA((CHUNKS,)),
        ],
        compiler_params=params(12),
        cost_estimate=cost(2 * tokens * model * key_width, 8 * MIB),
        name="grad",
    )(
        where, acts, gain, grads, inverse,
        own, over, own_got, over_got, peer_own, peer_first, peer_over, peer_own_first, peer_own_rest, peer_over_got,
    )
    peer_gains, input_grads = lax.optimization_barrier((peer_gains, input_grads))
    return input_grads, weight_grads.T, (gains + peer_gains).reshape(cols) / plan.groups


def by_collectives(activations, norm_gain, key_weight, key_grads):
    inputs = activations.astype(F32)
    inverse_rms = lax.rsqrt(jnp.mean(inputs * inputs, axis=1, keepdims=True) + EPS)
    normed = inputs * inverse_rms
    scaled = (normed * norm_gain).astype(BF16)
    grad_scaled = lax.dot_general(
        key_grads,
        lax.all_gather(key_weight, "sub", axis=0, tiled=True),
        (((1,), (1,)), ((), ())),
        preferred_element_type=F32,
    )
    gained = norm_gain * grad_scaled
    input_grads = (
        inverse_rms * (gained - normed * jnp.mean(gained * normed, axis=1, keepdims=True))
    ).astype(BF16)
    groups = lax.axis_size("grp")
    cols = key_weight.shape[0]
    rows = key_grads.shape[1] // groups
    term = lax.dot_general(
        key_grads, scaled, (((0,), (0,)), ((), ())), preferred_element_type=F32
    )
    received = lax.all_to_all(term, "grp", split_axis=0, concat_axis=1, tiled=True)
    shared = jnp.sum(received.reshape(rows, groups, scaled.shape[1]), axis=1)
    owned = lax.psum_scatter(shared, "sub", scatter_dimension=1, tiled=True).T
    summed = lax.psum(jnp.sum(grad_scaled * normed, axis=0), AXES)
    gain_sum = lax.dynamic_slice_in_dim(summed, lax.axis_index("sub") * cols, cols)
    return input_grads, owned / groups, gain_sum / groups


def local(groups, subs, activations, norm_gain, key_weight, key_grads):
    cols = key_weight.shape[0]
    rows = key_grads.shape[1] // groups
    if groups == 4 and subs % 2 == 0 and subs & (subs - 1) == 0 and cols % 128 == 0 and rows % 16 == 0:
        plan = Plan(groups, subs)
        return by_permutes(plan, activations, norm_gain, key_weight, key_grads)
    return by_collectives(activations, norm_gain, key_weight, key_grads)


def solution(mesh):
    return jax.shard_map(
        functools.partial(local, mesh.shape["grp"], mesh.shape["sub"]),
        mesh=mesh,
        in_specs=(P(AXES, None), P(), P("sub", None), P(AXES, None)),
        out_specs=(P(AXES, None), P("sub", "grp"), P("sub")),
        check_vma=False,
    )
```

```python
import functools

import jax
import jax.numpy as jnp
from jax import lax
from jax.experimental import pallas as pl
from jax.experimental.pallas import tpu as pltpu
from jax.sharding import PartitionSpec as P

AXES = ("grp", "sub")
EPS = 1e-05
F32 = jnp.float32
BF16 = jnp.bfloat16
MIB = 1024 * 1024
TILE = 16
CHUNKS = 4
EARLY = 1


def params(limit):
    return pltpu.CompilerParams(vmem_limit_bytes=limit * MIB)


def cost(flops, moved):
    return pl.CostEstimate(flops=0, bytes_accessed=0, transcendentals=0)


class Plan:
    def __init__(self, groups, subs):
        self.groups, self.subs = groups, subs
        self.width = groups // 2
        self.depth = subs // self.width

    def index(self, core, y, x, z):
        return (y * 2 + core) * self.subs + z * self.width + x

    def pairs(self, move):
        found = []
        for core in range(2):
            for y in range(self.width):
                for x in range(self.width):
                    for z in range(self.depth):
                        found.append((self.index(core, y, x, z), self.index(*move(core, y, x, z))))
        return found

    def send(self, array, move):
        return lax.ppermute(array, AXES, self.pairs(move))


def place(plan):
    grp, sub = lax.axis_index("grp"), lax.axis_index("sub")
    return grp % 2, grp // 2, sub % plan.width, sub // plan.width


def slot_of(plan, where, first, second, to_z):
    core = where[0]
    to_x = jnp.where(core == 0, second, first)
    to_y = jnp.where(core == 0, first, second)
    return (to_x * plan.depth + to_z) * plan.width + to_y


def first_and_second(where):
    core, y, x = where[0], where[1], where[2]
    return jnp.where(core == 0, y, x), jnp.where(core == 0, x, y)


def fetch(source, target, sem):
    copy = pltpu.make_async_copy(source, target, sem)
    copy.start()
    return copy


def fetch_rows(source, target, sems):
    chunk = target.shape[0] // CHUNKS
    parts = [pl.ds(part * chunk, chunk) for part in range(CHUNKS)]
    return [fetch(source.at[part], target.at[part], sems.at[k]) for k, part in enumerate(parts)]


def scale_rows(source, gain, scaled, start, stop):
    @pl.loop(0, (stop - start) // TILE, unroll=8)
    def _(step):
        part = pl.ds(pl.multiple_of(start + step * TILE, TILE), TILE)
        inputs = source[part, :].astype(F32)
        inverse_rms = lax.rsqrt(jnp.mean(inputs * inputs, axis=1, keepdims=True) + EPS)
        scaled[part, :] = (inputs * inverse_rms * gain[...]).astype(BF16)


def mine_kernel(
    plan, where, acts_ref, gain_ref, grads_ref, weight_ref,
    scaled, mine, other, piece, gain, acts, grads, weight, sems, ends,
):
    core = where[0]
    tokens = acts.shape[0]
    rows = grads.shape[1] // plan.groups
    load = fetch(gain_ref, gain, ends.at[0])
    loads = fetch_rows(acts_ref, acts, sems)
    grads_load = fetch(grads_ref, grads, ends.at[1])
    weight_load = fetch(weight_ref, weight, ends.at[2])
    load.wait()
    chunk = tokens // CHUNKS
    for part in range(CHUNKS):
        loads[part].wait()
        scale_rows(acts, gain, scaled, part * chunk, (part + 1) * chunk)
    grads_load.wait()
    for half, (even, odd) in enumerate(((mine, other), (other, mine))):

        @pl.when(core == half)
        def _():
            for part in range(plan.width):
                place = slice(part * rows, (part + 1) * rows)
                column = 2 * part * rows
                even[place, :] = grads[:, column : column + rows].T
                odd[place, :] = grads[:, column + rows : column + 2 * rows].T

    weight_load.wait()
    for number in range(plan.groups):

        @pl.when(where[1] * 2 + core == number)
        def _():
            piece[...] = weight[:, number * rows : (number + 1) * rows].T


def peer_kernel(plan, acts, gain, scaled):
    scale_rows(acts, gain, scaled, 0, acts.shape[0])


def term_kernel(
    plan, where, scaled, peer_scaled, mine, theirs, sent_ref, kept_ref, held_ref, totals,
):
    width, depth = plan.width, plan.depth
    rows = mine.shape[0] // width
    cols = scaled.shape[1] // plan.subs

    for to_x in range(width):
        for to_z in range(depth):
            column = (to_z * width + to_x) * cols
            here = slice(column, column + cols)
            total = jnp.dot(mine[...], scaled[:, here], preferred_element_type=F32)
            total += jnp.dot(theirs[...], peer_scaled[:, here], preferred_element_type=F32)
            slot = (to_x * depth + to_z) * width
            for to_y in range(width):
                totals[slot + to_y] = total[to_y * rows : (to_y + 1) * rows]

    first, mine_second = first_and_second(where)
    for to_z in range(depth):
        for second in range(width):
            slot = slot_of(plan, where, 1 - first, second, to_z)
            sent_ref[second * depth + to_z] = totals[pl.ds(slot, 1)][0].astype(BF16)
        for second, out_ref in ((1 - mine_second, kept_ref), (mine_second, held_ref)):
            out_ref[to_z] = totals[pl.ds(slot_of(plan, where, first, second, to_z), 1)][0]


def half_kernel(plan, where, kept, got_ref, sent_ref):
    _, second = first_and_second(where)
    for to_z in range(plan.depth):
        block = kept[to_z] + got_ref[pl.ds((1 - second) * plan.depth + to_z, 1)][0].astype(F32)
        sent_ref[to_z] = block.astype(BF16)


def pack_kernel(plan, *refs):
    for number, ref in enumerate(refs[:-1]):
        refs[-1][number] = ref[...]


def plane_kernel(plan, where, held, got_ref, own, again_ref, gain_ref, sums_ref, gains_ref, *sent_refs):
    _, second = first_and_second(where)
    rows, cols = sums_ref.shape
    for step in range(plan.depth):
        plane = where[3] ^ step
        block = held[pl.ds(plane, 1)] + got_ref[pl.ds(second * plan.depth + plane, 1)].astype(F32)
        block = (block + again_ref[pl.ds(plane, 1)].astype(F32))[0]
        gains = jnp.sum(block * own[step].astype(F32), axis=0, keepdims=True)
        gains = gains / gain_ref[:, columns(plan, where, 0, step, cols)]
        if step == 0:
            sums_ref[...] = block
            gains_ref[...] = gains
        else:
            sent_refs[step - 1][:rows, :] = block.astype(BF16)
            row = lax.broadcasted_iota(jnp.int32, (16, cols), 0)
            tail = jnp.zeros((16, cols), F32)
            for number in range(3):
                high = gains.astype(BF16).astype(F32)
                tail = jnp.where(row == number, high, tail)
                gains = gains - high
            sent_refs[step - 1][rows:, :] = tail.astype(BF16)


def last_kernel(plan, sums_ref, gains_ref, *refs):
    got_refs, (out_ref, out_gains_ref) = refs[:-2], refs[-2:]
    rows = sums_ref.shape[0]
    total, gains = sums_ref[...], gains_ref[...]
    for ref in got_refs:
        total = total + ref[:rows, :].astype(F32)
        gains = gains + jnp.sum(ref[rows:, :].astype(F32), axis=0, keepdims=True)
    out_ref[...] = total / plan.groups
    out_gains_ref[...] = gains


def columns(plan, where, flip, step, cols):
    sub = (where[3] ^ step) * plan.width + (where[2] ^ flip)
    return pl.ds(pl.multiple_of(sub * cols, cols), cols)


def load_kernel(plan, where, acts_ref, grads_ref, acts, grads, inverse, sems):
    load = fetch(grads_ref, grads, sems.at[2, 0])
    cols = acts.shape[-1]
    copies = [
        fetch(acts_ref.at[:, columns(plan, where, flip, step, cols)], acts.at[flip, step], sems.at[flip, step])
        for flip in range(2)
        for step in range(plan.depth)
    ]
    load.wait()
    tokens = grads.shape[0]
    for number, copy in enumerate(copies):
        copy.wait()
        block = acts.at[number // plan.depth, number % plan.depth]
        for start in range(0, tokens, TILE):
            part = slice(start, start + TILE)
            square = None
            for lane in range(0, cols, 128):
                inputs = block[part, lane : lane + 128].astype(F32)
                square = inputs * inputs if square is None else square + inputs * inputs
            if number == 0:
                inverse[part, :] = square
            else:
                inverse[part, :] += square
    mean_square = jnp.sum(inverse[...], axis=1, keepdims=True) / (2 * plan.depth * cols)
    inverse[...] = jnp.broadcast_to(lax.rsqrt(mean_square + EPS), inverse.shape)


def place_weight(plan, where, pieces, from_core, second, weight):
    depth = plan.depth
    blocks = [array.at[number] for array in pieces for number in range(array.shape[0])]
    rows = blocks[0].shape[0]
    for part in range(2):
        if second:
            flip = from_core if part == 0 else 1
            far_y = (1 - from_core) if part == 0 else 1
        else:
            flip = 0 if part == 0 else 1 - from_core
            far_y = 0 if part == 0 else from_core
        grp = (where[1] ^ far_y) * 2 + from_core
        here = pl.ds(pl.multiple_of(grp * rows, rows), rows)
        for step in range(depth):
            weight[pl.ds(flip * depth + step, 1), here] = blocks[part * depth + step][...][None]


def early_kernel(plan, where, grads, own, over, own_got, peer_own, partial, late_grads, weight):
    core, y = where[0], where[1]
    depth, rows = own.shape[:2]

    def place(grp, step, block):
        weight[step, pl.ds(pl.multiple_of(grp * rows, rows), rows)] = block

    missing = (1 - y) * 2 + 1 - core
    for step in range(depth):
        third = jnp.where(core == 0, own_got[step].astype(F32), over[step].astype(F32))
        place(y * 2 + core, step, own[step])
        place(y * 2 + 1 - core, step, peer_own[step])
        place((1 - y) * 2 + core, step, third.astype(BF16))
        place(missing, step, jnp.zeros(third.shape, BF16))
        partial[step] = jnp.dot(grads[...], weight[step], preferred_element_type=F32)
    for number in range(plan.groups):

        @pl.when(missing == number)
        def _():
            late_grads[...] = grads[:, number * rows : (number + 1) * rows]


def grad_kernel(
    plan, where, acts, gain_ref, grads, inverse, partial, late_grads,
    own, over, own_got, over_got, peer_own, peer_first, peer_over, peer_own_first, peer_own_rest, peer_over_got,
    out_ref, weight, grad_scaled, mean_ref, out, ends,
):
    core = where[0]
    depth = plan.depth
    tokens, cols = acts.shape[2:]
    model = cols * plan.subs
    place_weight(plan, where, [own, over], core, False, weight)
    place_weight(plan, where, [peer_own, peer_first, peer_over], 1 - core, False, weight)
    place_weight(plan, where, [own_got, over_got], core, True, weight)
    place_weight(plan, where, [peer_own_first, peer_own_rest, peer_over_got], 1 - core, True, weight)
    blocks = [(flip, step) for flip in range(2) for step in range(depth)]

    def multiply(number):
        if number < depth:
            rows = late_grads.shape[1]
            missing = (1 - where[1]) * 2 + 1 - core
            block = weight[number, pl.ds(pl.multiple_of(missing * rows, rows), rows)]
            late = jnp.dot(late_grads[...], block, preferred_element_type=F32)
            grad_scaled[number] = partial[number] + late
        else:
            grad_scaled[number] = jnp.dot(grads[...], weight[number], preferred_element_type=F32)

    def add_mean(number):
        flip, step = blocks[number]
        gain = gain_ref[:, columns(plan, where, flip, step, cols)]
        for start in range(0, tokens, TILE):
            part = slice(start, start + TILE)
            mean = None
            for lane in range(0, cols, 128):
                lanes = slice(lane, lane + 128)
                product = gain[:, lanes] * grad_scaled[number, part, lanes]
                product = product * acts[flip, step, part, lanes].astype(F32)
                mean = product if mean is None else mean + product
            if number == 0:
                mean_ref[part, :] = mean
            else:
                mean_ref[part, :] += mean

    multiply(0)
    for number in range(1, len(blocks)):
        multiply(number)
        add_mean(number - 1)
    add_mean(len(blocks) - 1)
    mean = jnp.sum(mean_ref[...], axis=1, keepdims=True) / model
    scale = inverse[...]
    mean_ref[...] = mean * scale * scale * scale

    stores = []
    big = tokens // CHUNKS
    for base in range(0, tokens, big):
        for flip, step in blocks:
            number = flip * depth + step
            here = columns(plan, where, flip, step, cols)
            gain = gain_ref[:, here]
            for start in range(base, base + big, TILE):
                part = slice(start, start + TILE)
                scale = inverse[part, :]
                mean = mean_ref[part, :]
                tiles = []
                for lane in range(0, cols, 128):
                    lanes = slice(lane, lane + 128)
                    inputs = acts[flip, step, part, lanes].astype(F32)
                    gained = gain[:, lanes] * grad_scaled[number, part, lanes]
                    tiles.append((scale * gained - inputs * mean).astype(BF16))
                out[part, here] = jnp.concatenate(tiles, axis=1)
        rows_here = pl.ds(base, big)
        stores.append(fetch(out.at[rows_here], out_ref.at[rows_here], ends.at[base // big]))
    for store in stores:
        store.wait()


SMEM = pl.BlockSpec(memory_space=pltpu.SMEM)
VMEM = pl.BlockSpec(memory_space=pltpu.VMEM)
HBM = pl.BlockSpec(memory_space=pltpu.HBM)


def by_permutes(plan, activations, norm_gain, key_weight, key_grads):
    tokens, model = activations.shape
    key_width = key_grads.shape[1]
    rows, cols = key_width // plan.groups, model // plan.subs
    width, depth = plan.width, plan.depth
    gain = norm_gain.reshape(1, model)
    core, y, x, z = place(plan)
    where = jnp.stack([core, y, x, z]).astype(jnp.int32)
    shape = jax.ShapeDtypeStruct

    def to_core(core, y, x, z):
        return 1 - core, y, x, z

    def to_x(core, y, x, z):
        return core, y, x ^ 1, z

    def to_y(core, y, x, z):
        return core, y ^ 1, x, z

    def to_z(step):
        return lambda core, y, x, z: (core, y, x, z ^ step)

    def y_then(core, y, x, z):
        return (core, y ^ 1, x, z) if core == 0 else (core, y, x ^ 1, z)

    def x_then(core, y, x, z):
        return (core, y, x ^ 1, z) if core == 0 else (core, y ^ 1, x, z)

    def in_hbm(array):
        return pltpu.with_memory_space_constraint(array, pltpu.HBM)

    acts_hbm, grads_hbm, gain_hbm = in_hbm(activations), in_hbm(key_grads), in_hbm(gain)

    peer_acts = plan.send(activations, to_core)
    half_shape = (width * rows, tokens)
    scaled, mine, other, piece, near_gain = pl.pallas_call(
        functools.partial(mine_kernel, plan),
        out_shape=(
            pltpu.VMEM((tokens, model), BF16),
            pltpu.VMEM(half_shape, BF16),
            pltpu.VMEM(half_shape, BF16),
            pltpu.VMEM((rows, cols), BF16),
            pltpu.VMEM((1, model), F32),
        ),
        in_specs=[SMEM, HBM, HBM, HBM, HBM],
        out_specs=[VMEM] * 5,
        scratch_shapes=[
            pltpu.VMEM((tokens, model), BF16),
            pltpu.VMEM((tokens, key_width), BF16),
            pltpu.VMEM((cols, key_width), BF16),
            pltpu.SemaphoreType.DMA((CHUNKS,)),
            pltpu.SemaphoreType.DMA((3,)),
        ],
        compiler_params=params(5),
        cost_estimate=cost(0, 8 * MIB),
        name="mine",
    )(where, acts_hbm, gain_hbm, grads_hbm, in_hbm(key_weight))
    theirs = plan.send(other, to_core)
    peer_scaled = pl.pallas_call(
        functools.partial(peer_kernel, plan),
        out_shape=pltpu.VMEM((tokens, model), BF16),
        in_specs=[VMEM, VMEM],
        out_specs=VMEM,
        compiler_params=params(2),
        cost_estimate=cost(0, 2 * MIB),
        name="peer",
    )(peer_acts, near_gain)
    theirs, _ = lax.optimization_barrier((theirs, peer_scaled))
    sent, kept, held = pl.pallas_call(
        functools.partial(term_kernel, plan),
        out_shape=(
            pltpu.VMEM((width * depth, rows, cols), BF16),
            pltpu.VMEM((depth, rows, cols), F32),
            pltpu.VMEM((depth, rows, cols), F32),
        ),
        in_specs=[SMEM] + [VMEM] * 4,
        out_specs=[VMEM] * 3,
        scratch_shapes=[pltpu.VMEM((2 * width * depth, rows, cols), F32)],
        compiler_params=params(6),
        cost_estimate=cost(4 * tokens * model * width * rows, 20 * MIB),
        name="term",
    )(where, scaled, peer_scaled, mine, theirs)
    got = plan.send(sent, y_then)

    acts, grads, inverse = pl.pallas_call(
        functools.partial(load_kernel, plan),
        out_shape=(
            pltpu.VMEM((2, depth, tokens, cols), BF16),
            pltpu.VMEM((tokens, key_width), BF16),
            pltpu.VMEM((tokens, 128), F32),
        ),
        in_specs=[SMEM, HBM, HBM],
        out_specs=[VMEM] * 3,
        scratch_shapes=[pltpu.SemaphoreType.DMA((3, depth))],
        compiler_params=params(1),
        cost_estimate=cost(0, 8 * MIB),
        name="load",
    )(where, acts_hbm, grads_hbm)

    planes = [plan.send(piece, to_z(step)) for step in range(1, depth)]
    got, planes[1], acts, grads, inverse = lax.optimization_barrier(
        (got, planes[1], acts, grads, inverse)
    )

    sent = pl.pallas_call(
        functools.partial(half_kernel, plan),
        out_shape=pltpu.VMEM((depth, rows, cols), BF16),
        in_specs=[SMEM, VMEM, VMEM],
        out_specs=VMEM,
        compiler_params=params(2),
        cost_estimate=cost(0, 2 * MIB),
        name="half",
    )(where, kept, got)
    sent, planes = lax.optimization_barrier((sent, planes))
    again = plan.send(sent, x_then)

    own = pl.pallas_call(
        functools.partial(pack_kernel, plan),
        out_shape=pltpu.VMEM((depth, rows, cols), BF16),
        in_specs=[VMEM] * depth,
        out_specs=VMEM,
        compiler_params=params(1),
        cost_estimate=cost(0, MIB),
        name="pack",
    )(piece, *planes)
    own, _ = lax.optimization_barrier((own, sent))
    over = plan.send(own, x_then)
    sums, gains, *sents = pl.pallas_call(
        functools.partial(plane_kernel, plan),
        out_shape=[pltpu.VMEM((rows, cols), F32), pltpu.VMEM((1, cols), F32)]
        + [pltpu.VMEM((rows + 16, cols), BF16)] * (depth - 1),
        in_specs=[SMEM] + [VMEM] * 5,
        out_specs=[VMEM] * (1 + depth),
        compiler_params=params(3),
        cost_estimate=cost(0, 2 * MIB),
        name="plane",
    )(where, held, got, own, again, gain)
    gots = [plan.send(array, to_z(step + 1)) for step, array in enumerate(sents)]
    peer_own = plan.send(own, to_core)
    first, _, peer_own = lax.optimization_barrier((own, again, peer_own))
    own_got = plan.send(first, y_then)
    over_got = plan.send(over, y_then)
    partial, late_grads = pl.pallas_call(
        functools.partial(early_kernel, plan),
        out_shape=(pltpu.VMEM((depth, tokens, cols), F32), pltpu.VMEM((tokens, rows), BF16)),
        in_specs=[SMEM] + [VMEM] * 5,
        out_specs=[VMEM] * 2,
        scratch_shapes=[pltpu.VMEM((depth, key_width, cols), BF16)],
        compiler_params=params(5),
        cost_estimate=cost(0, MIB),
        name="early",
    )(where, grads, own, over, own_got, peer_own)
    gots, partial = lax.optimization_barrier((gots, partial))
    weight_grads, gains = pl.pallas_call(
        functools.partial(last_kernel, plan),
        out_shape=(shape((rows, cols), F32), pltpu.VMEM((1, cols), F32)),
        in_specs=[VMEM] * (depth + 1),
        out_specs=(VMEM, VMEM),
        compiler_params=params(2),
        cost_estimate=cost(0, MIB),
        name="last",
    )(sums, gains, *gots)
    peer_first = plan.send(over[: 2 * EARLY], to_core)
    rest, gains = lax.optimization_barrier((over[2 * EARLY :], gains))
    peer_over = plan.send(rest, to_core)
    gains = gains + plan.send(gains, to_core)
    peer_own_first = plan.send(own_got[: depth - 1], to_core)
    over_got, peer_over, peer_own_first, gains = lax.optimization_barrier(
        (over_got, peer_over, peer_own_first, gains)
    )
    peer_over_got = plan.send(over_got, to_core)
    peer_own_rest = plan.send(own_got[depth - 1 :], to_core)
    peer_gains = plan.send(gains, to_y)

    input_grads = pl.pallas_call(
        functools.partial(grad_kernel, plan),
        out_shape=shape((tokens, model), BF16),
        in_specs=[SMEM] + [VMEM] * 16,
        out_specs=HBM,
        scratch_shapes=[
            pltpu.VMEM((2 * depth, key_width, cols), BF16),
            pltpu.VMEM((2 * depth, tokens, cols), F32),
            pltpu.VMEM((tokens, 128), F32),
            pltpu.VMEM((tokens, model), BF16),
            pltpu.SemaphoreType.DMA((CHUNKS,)),
        ],
        compiler_params=params(12),
        cost_estimate=cost(2 * tokens * model * key_width, 8 * MIB),
        name="grad",
    )(
        where, acts, gain, grads, inverse, partial, late_grads,
        own, over, own_got, over_got, peer_own, peer_first, peer_over, peer_own_first, peer_own_rest, peer_over_got,
    )
    peer_gains, input_grads = lax.optimization_barrier((peer_gains, input_grads))
    return input_grads, weight_grads.T, (gains + peer_gains).reshape(cols) / plan.groups


def by_collectives(activations, norm_gain, key_weight, key_grads):
    inputs = activations.astype(F32)
    inverse_rms = lax.rsqrt(jnp.mean(inputs * inputs, axis=1, keepdims=True) + EPS)
    normed = inputs * inverse_rms
    scaled = (normed * norm_gain).astype(BF16)
    grad_scaled = lax.dot_general(
        key_grads,
        lax.all_gather(key_weight, "sub", axis=0, tiled=True),
        (((1,), (1,)), ((), ())),
        preferred_element_type=F32,
    )
    gained = norm_gain * grad_scaled
    input_grads = (
        inverse_rms * (gained - normed * jnp.mean(gained * normed, axis=1, keepdims=True))
    ).astype(BF16)
    groups = lax.axis_size("grp")
    cols = key_weight.shape[0]
    rows = key_grads.shape[1] // groups
    term = lax.dot_general(
        key_grads, scaled, (((0,), (0,)), ((), ())), preferred_element_type=F32
    )
    received = lax.all_to_all(term, "grp", split_axis=0, concat_axis=1, tiled=True)
    shared = jnp.sum(received.reshape(rows, groups, scaled.shape[1]), axis=1)
    owned = lax.psum_scatter(shared, "sub", scatter_dimension=1, tiled=True).T
    summed = lax.psum(jnp.sum(grad_scaled * normed, axis=0), AXES)
    gain_sum = lax.dynamic_slice_in_dim(summed, lax.axis_index("sub") * cols, cols)
    return input_grads, owned / groups, gain_sum / groups


def local(groups, subs, activations, norm_gain, key_weight, key_grads):
    cols = key_weight.shape[0]
    rows = key_grads.shape[1] // groups
    if groups == 4 and subs % 2 == 0 and subs & (subs - 1) == 0 and cols % 128 == 0 and rows % 16 == 0:
        plan = Plan(groups, subs)
        return by_permutes(plan, activations, norm_gain, key_weight, key_grads)
    return by_collectives(activations, norm_gain, key_weight, key_grads)


def solution(mesh):
    return jax.shard_map(
        functools.partial(local, mesh.shape["grp"], mesh.shape["sub"]),
        mesh=mesh,
        in_specs=(P(AXES, None), P(), P("sub", None), P(AXES, None)),
        out_specs=(P(AXES, None), P("sub", "grp"), P("sub")),
        check_vma=False,
    )
```

```python
import functools

import jax
import jax.numpy as jnp
from jax import lax
from jax.experimental import pallas as pl
from jax.experimental.pallas import tpu as pltpu
from jax.sharding import PartitionSpec as P

AXES = ("grp", "sub")
EPS = 1e-05
F32 = jnp.float32
BF16 = jnp.bfloat16
MIB = 1024 * 1024
TILE = 16
CHUNKS = 4
EARLY = 1


def params(limit):
    return pltpu.CompilerParams(vmem_limit_bytes=limit * MIB)


def cost(flops, moved):
    return pl.CostEstimate(flops=0, bytes_accessed=0, transcendentals=0)


class Plan:
    def __init__(self, groups, subs):
        self.groups, self.subs = groups, subs
        self.width = groups // 2
        self.depth = subs // self.width

    def index(self, core, y, x, z):
        return (y * 2 + core) * self.subs + z * self.width + x

    def pairs(self, move):
        found = []
        for core in range(2):
            for y in range(self.width):
                for x in range(self.width):
                    for z in range(self.depth):
                        found.append((self.index(core, y, x, z), self.index(*move(core, y, x, z))))
        return found

    def send(self, array, move):
        return lax.ppermute(array, AXES, self.pairs(move))


def place(plan):
    grp, sub = lax.axis_index("grp"), lax.axis_index("sub")
    return grp % 2, grp // 2, sub % plan.width, sub // plan.width


def slot_of(plan, where, first, second, to_z):
    core = where[0]
    to_x = jnp.where(core == 0, second, first)
    to_y = jnp.where(core == 0, first, second)
    return (to_x * plan.depth + to_z) * plan.width + to_y


def first_and_second(where):
    core, y, x = where[0], where[1], where[2]
    return jnp.where(core == 0, y, x), jnp.where(core == 0, x, y)


def fetch(source, target, sem):
    copy = pltpu.make_async_copy(source, target, sem)
    copy.start()
    return copy


def fetch_rows(source, target, sems):
    chunk = target.shape[0] // CHUNKS
    parts = [pl.ds(part * chunk, chunk) for part in range(CHUNKS)]
    return [fetch(source.at[part], target.at[part], sems.at[k]) for k, part in enumerate(parts)]


def scale_rows(source, gain, scaled, start, stop):
    @pl.loop(0, (stop - start) // TILE, unroll=8)
    def _(step):
        part = pl.ds(pl.multiple_of(start + step * TILE, TILE), TILE)
        inputs = source[part, :].astype(F32)
        inverse_rms = lax.rsqrt(jnp.mean(inputs * inputs, axis=1, keepdims=True) + EPS)
        scaled[part, :] = (inputs * inverse_rms * gain[...]).astype(BF16)


def mine_kernel(
    plan, where, acts_ref, gain_ref, grads_ref, weight_ref,
    scaled, mine, other, piece, gain, acts, grads, weight, sems, ends,
):
    core = where[0]
    tokens = acts.shape[0]
    rows = grads.shape[1] // plan.groups
    load = fetch(gain_ref, gain, ends.at[0])
    loads = fetch_rows(acts_ref, acts, sems)
    grads_load = fetch(grads_ref, grads, ends.at[1])
    weight_load = fetch(weight_ref, weight, ends.at[2])
    load.wait()
    chunk = tokens // CHUNKS
    for part in range(CHUNKS):
        loads[part].wait()
        scale_rows(acts, gain, scaled, part * chunk, (part + 1) * chunk)
    grads_load.wait()
    for half, (even, odd) in enumerate(((mine, other), (other, mine))):

        @pl.when(core == half)
        def _():
            for part in range(plan.width):
                place = slice(part * rows, (part + 1) * rows)
                column = 2 * part * rows
                even[place, :] = grads[:, column : column + rows].T
                odd[place, :] = grads[:, column + rows : column + 2 * rows].T

    weight_load.wait()
    for number in range(plan.groups):

        @pl.when(where[1] * 2 + core == number)
        def _():
            piece[...] = weight[:, number * rows : (number + 1) * rows].T


def peer_kernel(plan, acts, gain, scaled):
    scale_rows(acts, gain, scaled, 0, acts.shape[0])


def term_kernel(
    plan, where, scaled, peer_scaled, mine, theirs, sent_ref, kept_ref, held_ref, totals,
):
    width, depth = plan.width, plan.depth
    rows = mine.shape[0] // width
    cols = scaled.shape[1] // plan.subs

    for to_x in range(width):
        for to_z in range(depth):
            column = (to_z * width + to_x) * cols
            here = slice(column, column + cols)
            total = jnp.dot(mine[...], scaled[:, here], preferred_element_type=F32)
            total += jnp.dot(theirs[...], peer_scaled[:, here], preferred_element_type=F32)
            slot = (to_x * depth + to_z) * width
            for to_y in range(width):
                totals[slot + to_y] = total[to_y * rows : (to_y + 1) * rows]

    first, mine_second = first_and_second(where)
    for to_z in range(depth):
        for second in range(width):
            slot = slot_of(plan, where, 1 - first, second, to_z)
            sent_ref[second * depth + to_z] = totals[pl.ds(slot, 1)][0].astype(BF16)
        for second, out_ref in ((1 - mine_second, kept_ref), (mine_second, held_ref)):
            out_ref[to_z] = totals[pl.ds(slot_of(plan, where, first, second, to_z), 1)][0]


def half_kernel(plan, where, kept, got_ref, sent_ref):
    _, second = first_and_second(where)
    for to_z in range(plan.depth):
        block = kept[to_z] + got_ref[pl.ds((1 - second) * plan.depth + to_z, 1)][0].astype(F32)
        sent_ref[to_z] = block.astype(BF16)


def pack_kernel(plan, *refs):
    for number, ref in enumerate(refs[:-1]):
        refs[-1][number] = ref[...]


def plane_kernel(plan, where, held, got_ref, own, again_ref, gain_ref, sums_ref, gains_ref, *sent_refs):
    _, second = first_and_second(where)
    rows, cols = sums_ref.shape
    for step in range(plan.depth):
        plane = where[3] ^ step
        block = held[pl.ds(plane, 1)] + got_ref[pl.ds(second * plan.depth + plane, 1)].astype(F32)
        block = (block + again_ref[pl.ds(plane, 1)].astype(F32))[0]
        gains = jnp.sum(block * own[step].astype(F32), axis=0, keepdims=True)
        gains = gains / gain_ref[:, columns(plan, where, 0, step, cols)]
        if step == 0:
            sums_ref[...] = block
            gains_ref[...] = gains
        else:
            sent_refs[step - 1][:rows, :] = block.astype(BF16)
            row = lax.broadcasted_iota(jnp.int32, (16, cols), 0)
            tail = jnp.zeros((16, cols), F32)
            for number in range(3):
                high = gains.astype(BF16).astype(F32)
                tail = jnp.where(row == number, high, tail)
                gains = gains - high
            sent_refs[step - 1][rows:, :] = tail.astype(BF16)


def last_kernel(plan, sums_ref, gains_ref, *refs):
    got_refs, (out_ref, out_gains_ref) = refs[:-2], refs[-2:]
    rows = sums_ref.shape[0]
    total, gains = sums_ref[...], gains_ref[...]
    for ref in got_refs:
        total = total + ref[:rows, :].astype(F32)
        gains = gains + jnp.sum(ref[rows:, :].astype(F32), axis=0, keepdims=True)
    out_ref[...] = total / plan.groups
    out_gains_ref[...] = gains


def columns(plan, where, flip, step, cols):
    sub = (where[3] ^ step) * plan.width + (where[2] ^ flip)
    return pl.ds(pl.multiple_of(sub * cols, cols), cols)


def load_kernel(plan, where, acts_ref, grads_ref, acts, grads, inverse, sems):
    load = fetch(grads_ref, grads, sems.at[2, 0])
    cols = acts.shape[-1]
    copies = [
        fetch(acts_ref.at[:, columns(plan, where, flip, step, cols)], acts.at[flip, step], sems.at[flip, step])
        for flip in range(2)
        for step in range(plan.depth)
    ]
    load.wait()
    tokens = grads.shape[0]
    for number, copy in enumerate(copies):
        copy.wait()
        block = acts.at[number // plan.depth, number % plan.depth]
        for start in range(0, tokens, TILE):
            part = slice(start, start + TILE)
            square = None
            for lane in range(0, cols, 128):
                inputs = block[part, lane : lane + 128].astype(F32)
                square = inputs * inputs if square is None else square + inputs * inputs
            if number == 0:
                inverse[part, :] = square
            else:
                inverse[part, :] += square
    mean_square = jnp.sum(inverse[...], axis=1, keepdims=True) / (2 * plan.depth * cols)
    inverse[...] = jnp.broadcast_to(lax.rsqrt(mean_square + EPS), inverse.shape)


def place_weight(plan, where, pieces, from_core, second, weight):
    depth = plan.depth
    blocks = [array.at[number] for array in pieces for number in range(array.shape[0])]
    rows = blocks[0].shape[0]
    for part in range(2):
        if second:
            flip = from_core if part == 0 else 1
            far_y = (1 - from_core) if part == 0 else 1
        else:
            flip = 0 if part == 0 else 1 - from_core
            far_y = 0 if part == 0 else from_core
        grp = (where[1] ^ far_y) * 2 + from_core
        here = pl.ds(pl.multiple_of(grp * rows, rows), rows)
        for step in range(depth):
            weight[pl.ds(flip * depth + step, 1), here] = blocks[part * depth + step][...][None]


def early_kernel(plan, where, grads, own, over, own_got, peer_own, partial, late_grads, weight):
    core, y = where[0], where[1]
    depth, rows = own.shape[:2]

    def place(grp, step, block):
        weight[step, pl.ds(pl.multiple_of(grp * rows, rows), rows)] = block

    missing = (1 - y) * 2 + 1 - core
    for step in range(depth):
        third = jnp.where(core == 0, own_got[step].astype(F32), over[step].astype(F32))
        place(y * 2 + core, step, own[step])
        place(y * 2 + 1 - core, step, peer_own[step])
        place((1 - y) * 2 + core, step, third.astype(BF16))
        place(missing, step, jnp.zeros(third.shape, BF16))
        partial[step] = jnp.dot(grads[...], weight[step], preferred_element_type=F32)
    for number in range(plan.groups):

        @pl.when(missing == number)
        def _():
            late_grads[...] = grads[:, number * rows : (number + 1) * rows]


def grad_kernel(
    plan, where, acts, gain_ref, grads, inverse, partial, late_grads,
    own, over, own_got, over_got, peer_own, peer_first, peer_over, peer_own_first, peer_over_got,
    out_ref, weight, grad_scaled, mean_ref, out, ends,
):
    core = where[0]
    depth = plan.depth
    tokens, cols = acts.shape[2:]
    model = cols * plan.subs
    place_weight(plan, where, [own, over], core, False, weight)
    place_weight(plan, where, [peer_own, peer_first, peer_over], 1 - core, False, weight)
    place_weight(plan, where, [own_got, over_got], core, True, weight)
    place_weight(plan, where, [peer_own_first, peer_over_got], 1 - core, True, weight)
    blocks = [(flip, step) for flip in range(2) for step in range(depth)]

    def multiply(number):
        if number < depth:
            rows = late_grads.shape[1]
            missing = (1 - where[1]) * 2 + 1 - core
            block = weight[number, pl.ds(pl.multiple_of(missing * rows, rows), rows)]
            late = jnp.dot(late_grads[...], block, preferred_element_type=F32)
            grad_scaled[number] = partial[number] + late
        else:
            grad_scaled[number] = jnp.dot(grads[...], weight[number], preferred_element_type=F32)

    def add_mean(number):
        flip, step = blocks[number]
        gain = gain_ref[:, columns(plan, where, flip, step, cols)]
        for start in range(0, tokens, TILE):
            part = slice(start, start + TILE)
            mean = None
            for lane in range(0, cols, 128):
                lanes = slice(lane, lane + 128)
                product = gain[:, lanes] * grad_scaled[number, part, lanes]
                product = product * acts[flip, step, part, lanes].astype(F32)
                mean = product if mean is None else mean + product
            if number == 0:
                mean_ref[part, :] = mean
            else:
                mean_ref[part, :] += mean

    multiply(0)
    for number in range(1, len(blocks)):
        multiply(number)
        add_mean(number - 1)
    add_mean(len(blocks) - 1)
    mean = jnp.sum(mean_ref[...], axis=1, keepdims=True) / model
    scale = inverse[...]
    mean_ref[...] = mean * scale * scale * scale

    stores = []
    big = tokens // CHUNKS
    for base in range(0, tokens, big):
        for flip, step in blocks:
            number = flip * depth + step
            here = columns(plan, where, flip, step, cols)
            gain = gain_ref[:, here]
            for start in range(base, base + big, TILE):
                part = slice(start, start + TILE)
                scale = inverse[part, :]
                mean = mean_ref[part, :]
                tiles = []
                for lane in range(0, cols, 128):
                    lanes = slice(lane, lane + 128)
                    inputs = acts[flip, step, part, lanes].astype(F32)
                    gained = gain[:, lanes] * grad_scaled[number, part, lanes]
                    tiles.append((scale * gained - inputs * mean).astype(BF16))
                out[part, here] = jnp.concatenate(tiles, axis=1)
        rows_here = pl.ds(base, big)
        stores.append(fetch(out.at[rows_here], out_ref.at[rows_here], ends.at[base // big]))
    for store in stores:
        store.wait()


SMEM = pl.BlockSpec(memory_space=pltpu.SMEM)
VMEM = pl.BlockSpec(memory_space=pltpu.VMEM)
HBM = pl.BlockSpec(memory_space=pltpu.HBM)


def by_permutes(plan, activations, norm_gain, key_weight, key_grads):
    tokens, model = activations.shape
    key_width = key_grads.shape[1]
    rows, cols = key_width // plan.groups, model // plan.subs
    width, depth = plan.width, plan.depth
    gain = norm_gain.reshape(1, model)
    core, y, x, z = place(plan)
    where = jnp.stack([core, y, x, z]).astype(jnp.int32)
    shape = jax.ShapeDtypeStruct

    def to_core(core, y, x, z):
        return 1 - core, y, x, z

    def to_x(core, y, x, z):
        return core, y, x ^ 1, z

    def to_y(core, y, x, z):
        return core, y ^ 1, x, z

    def to_z(step):
        return lambda core, y, x, z: (core, y, x, z ^ step)

    def y_then(core, y, x, z):
        return (core, y ^ 1, x, z) if core == 0 else (core, y, x ^ 1, z)

    def x_then(core, y, x, z):
        return (core, y, x ^ 1, z) if core == 0 else (core, y ^ 1, x, z)

    def in_hbm(array):
        return pltpu.with_memory_space_constraint(array, pltpu.HBM)

    acts_hbm, grads_hbm, gain_hbm = in_hbm(activations), in_hbm(key_grads), in_hbm(gain)

    peer_acts = plan.send(activations, to_core)
    half_shape = (width * rows, tokens)
    scaled, mine, other, piece, near_gain = pl.pallas_call(
        functools.partial(mine_kernel, plan),
        out_shape=(
            pltpu.VMEM((tokens, model), BF16),
            pltpu.VMEM(half_shape, BF16),
            pltpu.VMEM(half_shape, BF16),
            pltpu.VMEM((rows, cols), BF16),
            pltpu.VMEM((1, model), F32),
        ),
        in_specs=[SMEM, HBM, HBM, HBM, HBM],
        out_specs=[VMEM] * 5,
        scratch_shapes=[
            pltpu.VMEM((tokens, model), BF16),
            pltpu.VMEM((tokens, key_width), BF16),
            pltpu.VMEM((cols, key_width), BF16),
            pltpu.SemaphoreType.DMA((CHUNKS,)),
            pltpu.SemaphoreType.DMA((3,)),
        ],
        compiler_params=params(5),
        cost_estimate=cost(0, 8 * MIB),
        name="mine",
    )(where, acts_hbm, gain_hbm, grads_hbm, in_hbm(key_weight))
    theirs = plan.send(other, to_core)
    peer_scaled = pl.pallas_call(
        functools.partial(peer_kernel, plan),
        out_shape=pltpu.VMEM((tokens, model), BF16),
        in_specs=[VMEM, VMEM],
        out_specs=VMEM,
        compiler_params=params(2),
        cost_estimate=cost(0, 2 * MIB),
        name="peer",
    )(peer_acts, near_gain)
    theirs, _ = lax.optimization_barrier((theirs, peer_scaled))
    sent, kept, held = pl.pallas_call(
        functools.partial(term_kernel, plan),
        out_shape=(
            pltpu.VMEM((width * depth, rows, cols), BF16),
            pltpu.VMEM((depth, rows, cols), F32),
            pltpu.VMEM((depth, rows, cols), F32),
        ),
        in_specs=[SMEM] + [VMEM] * 4,
        out_specs=[VMEM] * 3,
        scratch_shapes=[pltpu.VMEM((2 * width * depth, rows, cols), F32)],
        compiler_params=params(6),
        cost_estimate=cost(4 * tokens * model * width * rows, 20 * MIB),
        name="term",
    )(where, scaled, peer_scaled, mine, theirs)
    got = plan.send(sent, y_then)

    acts, grads, inverse = pl.pallas_call(
        functools.partial(load_kernel, plan),
        out_shape=(
            pltpu.VMEM((2, depth, tokens, cols), BF16),
            pltpu.VMEM((tokens, key_width), BF16),
            pltpu.VMEM((tokens, 128), F32),
        ),
        in_specs=[SMEM, HBM, HBM],
        out_specs=[VMEM] * 3,
        scratch_shapes=[pltpu.SemaphoreType.DMA((3, depth))],
        compiler_params=params(1),
        cost_estimate=cost(0, 8 * MIB),
        name="load",
    )(where, acts_hbm, grads_hbm)

    planes = [plan.send(piece, to_z(step)) for step in range(1, depth)]
    got, planes[1], acts, grads, inverse = lax.optimization_barrier(
        (got, planes[1], acts, grads, inverse)
    )

    sent = pl.pallas_call(
        functools.partial(half_kernel, plan),
        out_shape=pltpu.VMEM((depth, rows, cols), BF16),
        in_specs=[SMEM, VMEM, VMEM],
        out_specs=VMEM,
        compiler_params=params(2),
        cost_estimate=cost(0, 2 * MIB),
        name="half",
    )(where, kept, got)
    sent, planes = lax.optimization_barrier((sent, planes))
    again = plan.send(sent, x_then)

    own = pl.pallas_call(
        functools.partial(pack_kernel, plan),
        out_shape=pltpu.VMEM((depth, rows, cols), BF16),
        in_specs=[VMEM] * depth,
        out_specs=VMEM,
        compiler_params=params(1),
        cost_estimate=cost(0, MIB),
        name="pack",
    )(piece, *planes)
    own, _ = lax.optimization_barrier((own, sent))
    over = plan.send(own, x_then)
    sums, gains, *sents = pl.pallas_call(
        functools.partial(plane_kernel, plan),
        out_shape=[pltpu.VMEM((rows, cols), F32), pltpu.VMEM((1, cols), F32)]
        + [pltpu.VMEM((rows + 16, cols), BF16)] * (depth - 1),
        in_specs=[SMEM] + [VMEM] * 5,
        out_specs=[VMEM] * (1 + depth),
        compiler_params=params(3),
        cost_estimate=cost(0, 2 * MIB),
        name="plane",
    )(where, held, got, own, again, gain)
    gots = [plan.send(array, to_z(step + 1)) for step, array in enumerate(sents)]
    peer_own = plan.send(own, to_core)
    first, _, peer_own = lax.optimization_barrier((own, again, peer_own))
    own_got = plan.send(first, y_then)
    over_got = plan.send(over, y_then)
    partial, late_grads = pl.pallas_call(
        functools.partial(early_kernel, plan),
        out_shape=(pltpu.VMEM((depth, tokens, cols), F32), pltpu.VMEM((tokens, rows), BF16)),
        in_specs=[SMEM] + [VMEM] * 5,
        out_specs=[VMEM] * 2,
        scratch_shapes=[pltpu.VMEM((depth, key_width, cols), BF16)],
        compiler_params=params(5),
        cost_estimate=cost(0, MIB),
        name="early",
    )(where, grads, own, over, own_got, peer_own)
    gots, partial = lax.optimization_barrier((gots, partial))
    weight_grads, gains = pl.pallas_call(
        functools.partial(last_kernel, plan),
        out_shape=(shape((rows, cols), F32), pltpu.VMEM((1, cols), F32)),
        in_specs=[VMEM] * (depth + 1),
        out_specs=(VMEM, VMEM),
        compiler_params=params(2),
        cost_estimate=cost(0, MIB),
        name="last",
    )(sums, gains, *gots)
    peer_first = plan.send(over[: 2 * EARLY], to_core)
    rest, gains = lax.optimization_barrier((over[2 * EARLY :], gains))
    peer_over = plan.send(rest, to_core)
    gains = gains + plan.send(gains, to_core)
    peer_own_first = plan.send(own_got, to_core)
    over_got, peer_over, peer_own_first, gains = lax.optimization_barrier(
        (over_got, peer_over, peer_own_first, gains)
    )
    peer_over_got = plan.send(over_got, to_core)
    peer_gains = plan.send(gains, to_y)

    input_grads = pl.pallas_call(
        functools.partial(grad_kernel, plan),
        out_shape=shape((tokens, model), BF16),
        in_specs=[SMEM] + [VMEM] * 15,
        out_specs=HBM,
        scratch_shapes=[
            pltpu.VMEM((2 * depth, key_width, cols), BF16),
            pltpu.VMEM((2 * depth, tokens, cols), F32),
            pltpu.VMEM((tokens, 128), F32),
            pltpu.VMEM((tokens, model), BF16),
            pltpu.SemaphoreType.DMA((CHUNKS,)),
        ],
        compiler_params=params(12),
        cost_estimate=cost(2 * tokens * model * key_width, 8 * MIB),
        name="grad",
    )(
        where, acts, gain, grads, inverse, partial, late_grads,
        own, over, own_got, over_got, peer_own, peer_first, peer_over, peer_own_first, peer_over_got,
    )
    peer_gains, input_grads = lax.optimization_barrier((peer_gains, input_grads))
    return input_grads, weight_grads.T, (gains + peer_gains).reshape(cols) / plan.groups


def by_collectives(activations, norm_gain, key_weight, key_grads):
    inputs = activations.astype(F32)
    inverse_rms = lax.rsqrt(jnp.mean(inputs * inputs, axis=1, keepdims=True) + EPS)
    normed = inputs * inverse_rms
    scaled = (normed * norm_gain).astype(BF16)
    grad_scaled = lax.dot_general(
        key_grads,
        lax.all_gather(key_weight, "sub", axis=0, tiled=True),
        (((1,), (1,)), ((), ())),
        preferred_element_type=F32,
    )
    gained = norm_gain * grad_scaled
    input_grads = (
        inverse_rms * (gained - normed * jnp.mean(gained * normed, axis=1, keepdims=True))
    ).astype(BF16)
    groups = lax.axis_size("grp")
    cols = key_weight.shape[0]
    rows = key_grads.shape[1] // groups
    term = lax.dot_general(
        key_grads, scaled, (((0,), (0,)), ((), ())), preferred_element_type=F32
    )
    received = lax.all_to_all(term, "grp", split_axis=0, concat_axis=1, tiled=True)
    shared = jnp.sum(received.reshape(rows, groups, scaled.shape[1]), axis=1)
    owned = lax.psum_scatter(shared, "sub", scatter_dimension=1, tiled=True).T
    summed = lax.psum(jnp.sum(grad_scaled * normed, axis=0), AXES)
    gain_sum = lax.dynamic_slice_in_dim(summed, lax.axis_index("sub") * cols, cols)
    return input_grads, owned / groups, gain_sum / groups


def local(groups, subs, activations, norm_gain, key_weight, key_grads):
    cols = key_weight.shape[0]
    rows = key_grads.shape[1] // groups
    if groups == 4 and subs % 2 == 0 and subs & (subs - 1) == 0 and cols % 128 == 0 and rows % 16 == 0:
        plan = Plan(groups, subs)
        return by_permutes(plan, activations, norm_gain, key_weight, key_grads)
    return by_collectives(activations, norm_gain, key_weight, key_grads)


def solution(mesh):
    return jax.shard_map(
        functools.partial(local, mesh.shape["grp"], mesh.shape["sub"]),
        mesh=mesh,
        in_specs=(P(AXES, None), P(), P("sub", None), P(AXES, None)),
        out_specs=(P(AXES, None), P("sub", "grp"), P("sub")),
        check_vma=False,
    )
```
